512 devices in a mesh: section: 16 (over y, x), expert: 32 (over z, core).
Axes of the slice: x: 4, y: 4, z: 16, core: 2. Of those that a mesh axis runs over, the one named last changes fastest.
Arguments:
- in_flight: bfloat16 [16, 2, 1024, 1024], P('section', None, 'expert'), may hold values from -6 to 6
- arriving: bfloat16 [1, 2, 1024, 1024], P(None, None, 'expert'), may hold values from -6 to 6
- norm_gain: float32 [16, 1024], P('section'), may hold values from 0.1 to 1.9
- gate_up: bfloat16 [16, 32, 1024, 1536], P('section', 'expert'), may hold values from -0.1875 to 0.1875
- w_down: bfloat16 [16, 32, 768, 1024], P('section', 'expert'), may hold values from -0.21875 to 0.21875
- expert_ids: int32 [2, 16, 2, 1024, 8], P(None, 'section', None, 'expert'), may hold values from 0 to 31, all different within a row; in each aligned block of 32 rows (0 to 31, 32 to 63, ..., all dimensions but the last counted through in order) at most 16 rows name the same one
- route_weights: float32 [2, 16, 2, 1024, 8], P(None, 'section', None, 'expert'), may hold values from 0.05 to 1
Outputs:
- section_outputs: bfloat16 [2, 16, 2, 1024, 1024], P(None, 'section', None, 'expert')
The draws below stay inside these ranges and needn't reach their ends.
Inputs may be any that keep to these rules, and one draw needn't show every extreme that they name: `expert_ids`: each token names 8 different experts. In each micro-batch of each step and section, the tokens of one aligned block of 32 (the rows of one device) name one expert at most 16 times.
All inputs are finite; a program needn't handle non-finite values.
Results may differ from the reference program's by a relative error of at most 0.007.
Values may be sent and summed in bfloat16 or wider, within the bound.
A program may use at most 64 MiB of HBM per device.

```python
import math
import jax
import jax.numpy as jnp
import numpy as np
from jax import lax

D = 1024
FF = 768
TOPK = 8
MICRO = 2
TICKS = 2
MB_TOK = 32
EXPERTS = 32
TOKENS_MB = 1024
CAP = 16
N_SECTION = 16


def steps_of(stream_key, shape, cuts, smallest, high):
    loudness, own = 1.0, jax.random.fold_in(stream_key, 6)
    for position, shards_of in cuts:
        heights = jnp.exp(jax.random.uniform(jax.random.fold_in(own, position), (shards_of,), jnp.float32, smallest / len(cuts), high / len(cuts)))
        loudness = loudness * jnp.repeat(heights, shape[position] // shards_of).reshape([-1 if axis == position else 1 for axis in range(len(shape))])
    return loudness


def assign_block(own_key, own, number, rows, amount, top, limit, lean):
    sequence = jax.random.permutation(own_key, amount)
    heavy_load, common = portions_of(amount, rows * top, limit, lean, True), portions_of(amount, rows * top, limit, lean, False)
    places = jnp.arange(amount)

    def named(sizes, turn):
        used = int((sizes > 0).sum())
        fixed = max(1, used // 4)
        shifted = fixed + (places - fixed + turn * (used - fixed)) % max(1, amount - fixed)
        return jnp.zeros((amount,), jnp.int32).at[sequence[jnp.where(places < fixed, places, shifted)]].set(jnp.asarray(sizes, jnp.int32))

    sizes = jnp.where(number % 4 == 0, named(heavy_load, number // 4), named(common, number - number // 4 - 1))
    mixed = jax.random.permutation(jax.random.fold_in(own, 3), amount)
    donor, taker = mixed[0:amount // 2 * 2:2], mixed[1:amount // 2 * 2:2]
    margin = jnp.minimum(sizes[donor] - 1, limit - sizes[taker]) // 2
    margin = jnp.where((donor == sequence[0]) | (taker == sequence[0]) | (sizes[taker] == 0), 0, jnp.maximum(margin, 0))
    shifted = jax.random.randint(jax.random.fold_in(own, 4), (amount // 2,), 0, 1 << 20) % (margin + 1)
    sizes = sizes.at[donor].add(-shifted).at[taker].add(shifted)
    items = jnp.searchsorted(jnp.cumsum(sizes), jnp.arange(rows * top), side="right").astype(jnp.int32)
    grid = items.reshape(top, rows).T
    grid = grid[jax.random.permutation(jax.random.fold_in(own, 1), rows)]
    turn = jax.random.randint(jax.random.fold_in(own, 2), (rows, 1), 0, top)
    return jnp.take_along_axis(grid, (jnp.arange(top)[None, :] + turn) % top, axis=1)


def portions_of(count, total, reach, slope, full):
    loads = [(1 << 20) // math.isqrt(grade ** slope) + 1 for grade in range(1, count + 1)]
    largest = reach if full else min(reach, max(-(-total // count), total * loads[0] // sum(loads)))
    least = 1 if total - largest >= count - 1 else 0
    counts, spare = [largest] + [least] * (count - 1), total - largest - least * (count - 1)
    while spare > 0:
        candidates = [i for i in range(1, count) if counts[i] < largest] or [i for i in range(1, count) if counts[i] < reach]
        mass, budget = sum([loads[i] for i in candidates]), spare
        for i in candidates:
            extra = min(reach - counts[i], max(1, budget * loads[i] // mass), spare)
            counts[i] = counts[i] + extra
            spare = spare - extra
    return np.array(counts)


def scatter_about(key, shape, deviation, reach, split=(), kind=jnp.bfloat16):
    entries = jax.random.normal(key, shape, jnp.float32) * deviation
    if len(split) > 0:
        entries = steps_of(key, shape, split, -0.22, 0.18) * entries
    return jnp.clip(entries, min=-reach, max=reach).astype(kind)


def setup_inputs(seed: int = 0) -> dict:
    streams_of = jax.random.split(jax.random.key(seed), 8)
    in_flight = scatter_about(streams_of[0], (N_SECTION, MICRO, TOKENS_MB, D), 1.0, 6.0, ((0, 16), (2, 32)))
    arriving = scatter_about(streams_of[1], (TICKS - 1, MICRO, TOKENS_MB, D), 1.0, 6.0, ((2, 32),))
    norm_gain = jnp.clip(1.0 + 0.18 * jax.random.normal(streams_of[2], (N_SECTION, D), jnp.float32), 0.1, 1.9)
    gate_up = scatter_about(streams_of[3], (N_SECTION, EXPERTS, D, 2 * FF), D ** -0.5, 0.1875, ((0, 16), (1, 32)))
    w_down = scatter_about(streams_of[4], (N_SECTION, EXPERTS, FF, D), FF ** -0.5, 0.21875, ((0, 16), (1, 32)))
    expert_ids_keys = jax.random.split(jax.random.fold_in(streams_of[5], 1), TICKS * N_SECTION * MICRO * TOKENS_MB // MB_TOK)
    expert_ids_turns = jax.random.permutation(jax.random.fold_in(streams_of[5], 3), TICKS * N_SECTION * MICRO * TOKENS_MB // MB_TOK)
    expert_ids = jax.vmap(lambda own, number: assign_block(jax.random.fold_in(streams_of[5], 2), own, number, MB_TOK, EXPERTS, TOPK, CAP, 2))(expert_ids_keys, expert_ids_turns).reshape((TICKS, N_SECTION, MICRO, TOKENS_MB, TOPK))
    route_weights = jnp.clip(jnp.exp(math.log(1.0) - 2.9957323 * jax.random.uniform(streams_of[6], (TICKS, N_SECTION, MICRO, TOKENS_MB, TOPK), jnp.float32) ** steps_of(streams_of[6], (TICKS, N_SECTION, MICRO, TOKENS_MB, TOPK), ((1, 16), (3, 32)), -0.2, 0.2)), 0.05, 1.0)
    return dict(in_flight=in_flight, arriving=arriving, norm_gain=norm_gain, gate_up=gate_up, w_down=w_down, expert_ids=expert_ids, route_weights=route_weights)


def moe_layer(inflow, gain_row, gate_proj, down_proj, choice_ids, choice_weights):
    widened = inflow.astype(jnp.float32)
    inverse_rms = lax.rsqrt(lax.optimization_barrier(jnp.mean(widened * widened, axis=-1, keepdims=True)) + 1e-06)
    normed = (widened * inverse_rms * gain_row[None, :].astype(jnp.float32)).astype(jnp.bfloat16)
    blocks = TOKENS_MB // MB_TOK
    flat_ids = choice_ids.reshape(blocks, MB_TOK * TOPK).astype(jnp.int32)
    onehot = (flat_ids[:, :, None] == jnp.arange(EXPERTS, dtype=jnp.int32)[None, None, :]).astype(jnp.int32)
    earlier = jnp.cumsum(onehot, axis=1) - onehot
    slot_of = lax.optimization_barrier(jnp.sum(earlier * onehot, axis=-1)).astype(jnp.int32)
    row_index = (jnp.arange(blocks, dtype=jnp.int32)[:, None] * CAP + slot_of).reshape(-1)
    chosen = flat_ids.reshape(-1)
    token_index = jnp.arange(TOKENS_MB * TOPK, dtype=jnp.int32) // TOPK
    buffer = jnp.zeros((EXPERTS, blocks * CAP, D), jnp.bfloat16).at[chosen, row_index].set(normed[token_index])

    def one_expert(pieces):
        rows_in, w_in, w_out = pieces
        projected = jnp.dot(rows_in, w_in, preferred_element_type=jnp.float32)
        hidden = (jax.nn.silu(projected[:, :FF]) * projected[:, FF:]).astype(jnp.bfloat16)
        return jnp.dot(hidden, w_out, preferred_element_type=jnp.float32).astype(jnp.bfloat16)
    expert_out = lax.map(one_expert, (buffer, gate_proj, down_proj))
    picked = expert_out[chosen, row_index].reshape(TOKENS_MB, TOPK, D).astype(jnp.float32)
    branch = lax.optimization_barrier(jnp.sum(picked * choice_weights.astype(jnp.float32)[:, :, None], axis=1))
    return (widened + branch).astype(jnp.bfloat16)

def reference(in_flight, arriving, norm_gain, gate_up, w_down, expert_ids, route_weights):
    results = []
    inflow = in_flight
    for step_number in range(TICKS):
        if step_number > 0:
            inflow = jnp.concatenate([arriving[step_number - 1][None], results[-1][:-1]], axis=0)

        def one_section(pieces):
            section_in, gain_row, gate_proj, down_proj, section_ids, section_weights = pieces
            return jnp.stack([moe_layer(section_in[index], gain_row, gate_proj, down_proj, section_ids[index], section_weights[index]) for index in range(MICRO)])
        results.append(lax.map(one_section, (inflow, norm_gain, gate_up, w_down, expert_ids[step_number], route_weights[step_number])))
    return jnp.stack(results)
```

```python
import jax
import jax.numpy as jnp
from jax import lax
from jax.sharding import PartitionSpec as P


def shifted(value, axis, by):
    size = lax.axis_size(axis)
    pairs = [(i, i + by) for i in range(size) if 0 <= i + by < size]
    return lax.ppermute(value, axis, pairs)


def normalize(inflow, gain_row):
    widened = inflow.astype(jnp.float32)
    inverse_rms = lax.rsqrt(jnp.mean(widened * widened, axis=-1, keepdims=True) + 1e-06)
    return (widened * inverse_rms * gain_row).astype(jnp.bfloat16)


def local(in_flight, arriving, norm_gain, gate_up, w_down, expert_ids, route_weights):
    experts_all = lax.axis_size("expert") * gate_up.shape[1]
    hidden_count = w_down.shape[2]
    micro_count, tokens, features = in_flight.shape[1:]
    steps = expert_ids.shape[0]
    is_first = lax.axis_index("section") == 0
    gain_row = norm_gain[0][None, None, :]
    named = expert_ids[:, 0, ..., None] == jnp.arange(experts_all, dtype=jnp.int32)
    dense = jnp.sum(jnp.where(named, route_weights[:, 0, ..., None], 0.0), axis=3)
    dense = lax.all_to_all(dense, "expert", split_axis=3, concat_axis=2, tiled=True)
    outputs = []
    inflow = in_flight[0]
    for step_number in range(steps):
        if step_number > 0:
            incoming = shifted(outputs[-1], "section", 1)
            inflow = jnp.where(is_first, arriving[step_number - 1], incoming)
        normed = normalize(inflow, gain_row)
        everyone = lax.all_gather(normed, "expert", axis=1, tiled=True)
        rows = everyone.reshape(-1, features)
        projected = jnp.dot(rows, gate_up[0, 0], preferred_element_type=jnp.float32)
        hidden = (
            jax.nn.silu(projected[:, :hidden_count]) * projected[:, hidden_count:]
        ).astype(jnp.bfloat16)
        result = jnp.dot(hidden, w_down[0, 0], preferred_element_type=jnp.float32)
        share = (result.reshape(everyone.shape) * dense[step_number]).astype(jnp.bfloat16)
        branch = lax.psum_scatter(share, "expert", scatter_dimension=1, tiled=True)
        outputs.append((inflow.astype(jnp.float32) + branch.astype(jnp.float32)).astype(jnp.bfloat16))
    return jnp.stack(outputs)[:, None]


def solution(mesh):
    return jax.shard_map(
        local,
        mesh=mesh,
        in_specs=(
            P("section", None, "expert", None),
            P(None, None, "expert", None),
            P("section", None),
            P("section", "expert", None, None),
            P("section", "expert", None, None),
            P(None, "section", None, "expert", None),
            P(None, "section", None, "expert", None),
        ),
        out_specs=P(None, "section", None, "expert", None),
        check_vma=False,
    )
```

```python
import functools

import jax
import jax.numpy as jnp
from jax import lax
from jax.experimental import pallas as pl
from jax.experimental.pallas import tpu as pltpu
from jax.sharding import PartitionSpec as P

MESH = pl.DeviceIdType.MESH
LANES = 128


def relay_kernel(
    chips,
    sections,
    in_flight,
    arriving,
    norm_gain,
    gate_up,
    w_down,
    expert_ids,
    route_weights,
    out,
    rows0,
    rows1,
    sum_in,
    sum_out,
    part_out,
    part_in,
    own,
    home,
    inflow,
    entering,
    shifted,
    results,
    hidden,
    shares,
    gain,
    up_weights,
    down_weights,
    ids,
    weights,
    load_sems,
    swap_send,
    swap_recv,
    row_send,
    row_recv,
    mate_send,
    mate_recv,
    sum_send,
    sum_recv,
    part_send,
    part_recv,
    shift_send,
    shift_recv,
    out_send,
    out_recv,
    out_sems,
):
    steps, micros, tokens, top_count = expert_ids.shape[0], *expert_ids.shape[2:]
    features = in_flight.shape[-1]
    ff = w_down.shape[2]
    group = 2 * tokens
    tile = min(256, ff)
    experts = 2 * chips

    me = lax.axis_index("expert")
    section = lax.axis_index("section")
    core = lax.rem(me, 2)
    mate = me + 1 - 2 * core
    ahead = lax.rem(me + 2 - 4 * core + experts, experts)
    behind = lax.rem(me - 2 + 4 * core + experts, experts)
    section_after = lax.rem(section + 1, sections)
    section_before = lax.rem(section + sections - 1, sections)
    mine = pl.ds(pl.multiple_of(core * tokens, tokens), tokens)
    other = pl.ds(pl.multiple_of((1 - core) * tokens, tokens), tokens)

    loads = [
        pltpu.make_async_copy(source, target, load_sems.at[i])
        for i, (source, target) in enumerate(
            (
                (expert_ids, ids),
                (route_weights, weights),
                (norm_gain, gain),
                (in_flight.at[0, core], inflow.at[0, mine]),
                (arriving.at[0, core], entering.at[mine]),
                (gate_up.at[0, 0], up_weights),
                (w_down.at[0, 0], down_weights),
            )
        )
    ]
    for load in loads:
        load.start()

    barrier = pltpu.get_barrier_semaphore()
    for neighbour in (ahead, behind, mate):
        pl.semaphore_signal(barrier, inc=1, device_id={"expert": neighbour}, device_id_type=MESH)
    for neighbour in (section_after, section_before):
        pl.semaphore_signal(barrier, inc=1, device_id={"section": neighbour}, device_id_type=MESH)

    loads[0].wait()
    loads[1].wait()
    lane = lax.broadcasted_iota(jnp.int32, (tokens, LANES), 1)
    for micro in range(micros):
        dense = []
        for step in range(steps):
            step_ids, step_weights = ids[step, 0, micro], weights[step, 0, micro]
            total = jnp.zeros((tokens, LANES), jnp.float32)
            for k in range(top_count):
                named = step_ids[:, k : k + 1] == lax.rem(lane, experts)
                total = total + jnp.where(named, step_weights[:, k : k + 1], 0.0)
            dense.append(total)
        both = jnp.where(lane < 2 * experts, dense[0], dense[1])
        high = both.astype(jnp.bfloat16).astype(jnp.float32)
        is_high = lax.rem(lane, 2 * experts) < experts
        shares[micro] = jnp.where(is_high, high, both - high).astype(jnp.bfloat16)

    pl.semaphore_wait(barrier, 5)

    def swap(index, source, target):
        return pltpu.make_async_remote_copy(
            source, target, swap_send.at[index], swap_recv.at[index], {"expert": mate}, MESH
        )

    swaps = (
        swap(0, in_flight.at[0, 1 - core], inflow.at[0, mine]),
        swap(1, shares.at[1 - core], rows0.at[0, mine, pl.ds(features, LANES)]),
        swap(2, arriving.at[0, 1 - core], entering.at[mine]),
    )
    for copy in swaps:
        copy.start()
    rows0[0, mine, pl.ds(features, LANES)] = shares[core]
    sum_in[:, 1] = jnp.zeros((steps,) + sum_in.shape[2:], sum_in.dtype)

    mate_lane = lax.broadcasted_iota(jnp.int32, (2 * group, LANES), 1)

    def relay_step(step, rows):
        width = rows.shape[-1]

        def pass_on(k):
            return pltpu.make_async_remote_copy(
                rows.at[k, pl.ds(0, group)],
                rows.at[k + 1, pl.ds(0, group)],
                row_send.at[step],
                row_recv.at[step, k + 1],
                {"expert": ahead},
                MESH,
            )

        def to_mate(k):
            return pltpu.make_async_remote_copy(
                rows.at[k, pl.ds(0, group)],
                rows.at[k, pl.ds(group, group)],
                mate_send.at[step],
                mate_recv.at[step, k],
                {"expert": mate},
                MESH,
            )

        def part_to_mate(k):
            return pltpu.make_async_remote_copy(
                part_out.at[step, k],
                part_in.at[step, k],
                part_send.at[step],
                part_recv.at[step, k],
                {"expert": mate},
                MESH,
            )

        def sum_on(k):
            return pltpu.make_async_remote_copy(
                sum_out.at[step, k],
                sum_in.at[step, k + 1],
                sum_send.at[step],
                sum_recv.at[step, k + 1],
                {"expert": ahead},
                MESH,
            )

        def forward(k):
            @pl.when(k < chips - 1)
            def _():
                pass_on(k).start()

            to_mate(k).start()

        def multiply(k):
            to_mate(k).wait_recv()
            slot = lax.rem(k, 2)
            at = step * 2 * experts + me
            picked = (mate_lane == at) | (mate_lane == at + experts)
            share = rows0[k, :, pl.ds(features, LANES)].astype(jnp.float32)
            share = jnp.sum(jnp.where(picked, share, 0.0), axis=1, keepdims=True)
            block = rows[k, :, pl.ds(0, features)]
            for start in range(0, ff, tile):
                gate = jnp.dot(
                    block, up_weights[:, start : start + tile], preferred_element_type=jnp.float32
                )
                lift = jnp.dot(
                    block,
                    up_weights[:, ff + start : ff + start + tile],
                    preferred_element_type=jnp.float32,
                )
                hidden[:, start : start + tile] = (gate / (1.0 + jnp.exp(-gate)) * lift).astype(
                    jnp.bfloat16
                )
            for start in range(0, features, tile):
                result = jnp.dot(
                    hidden[...],
                    down_weights[:, start : start + tile],
                    preferred_element_type=jnp.float32,
                )
                result = result.astype(jnp.bfloat16).astype(jnp.float32) * share
                own[slot, :, start : start + tile] = result[:group]
                part_out[step, k, :, start : start + tile] = result[group:].astype(jnp.bfloat16)
            part_to_mate(k).start()

        def add(k):
            part_to_mate(k).wait_recv()
            slot = lax.rem(k, 2)
            both = own[slot] + part_in[step, k].astype(jnp.float32)

            @pl.when(k == 0)
            def _():
                home[...] = both + inflow[step].astype(jnp.float32)

            @pl.when(k > 0)
            def _():
                @pl.when(k > 1)
                def _():
                    sum_on(k - 1).wait_recv()

                sum_out[step, k] = (both + sum_in[step, k].astype(jnp.float32)).astype(jnp.bfloat16)
                sum_on(k).start()

        forward(0)

        def turn(k, carry):
            @pl.when(k < chips)
            def _():
                pass_on(k - 1).wait_recv()
                forward(k)

            multiply(k - 1)

            @pl.when(k > 1)
            def _():
                add(k - 2)

            return carry

        lax.fori_loop(1, chips + 1, turn, 0)
        add(chips - 1)
        sum_on(chips - 1).wait_recv()
        results[step] = (home[...] + sum_in[step, chips].astype(jnp.float32)).astype(jnp.bfloat16)

    def normalize(step, rows):
        wide = inflow[step].astype(jnp.float32)
        inverse = lax.rsqrt(jnp.mean(wide * wide, axis=-1, keepdims=True) + 1e-06)
        rows[0, pl.ds(0, group), pl.ds(0, features)] = (wide * inverse * gain[...]).astype(
            jnp.bfloat16
        )

    def hand_out(step):
        local = pltpu.make_async_copy(
            results.at[step, mine], out.at[step, 0, core], out_sems.at[step]
        )
        remote = pltpu.make_async_remote_copy(
            results.at[step, other],
            out.at[step, 0, core],
            out_send.at[step],
            out_recv.at[step],
            {"expert": mate},
            MESH,
        )
        return local, remote

    loads[2].wait()
    loads[3].wait()
    swaps[0].wait_recv()
    swaps[1].wait_recv()
    normalize(0, rows0)
    for load in loads[4:]:
        load.wait()
    relay_step(0, rows0)
    relay = pltpu.make_async_remote_copy(
        results.at[0], shifted, shift_send, shift_recv, {"section": section_after}, MESH
    )
    relay.start()
    for copy in hand_out(0):
        copy.start()
    swaps[2].wait_recv()
    relay.wait_recv()
    inflow[1] = jnp.where(section == 0, entering[...], shifted[...])
    normalize(1, rows1)
    relay_step(1, rows1)
    for copy in hand_out(1):
        copy.start()

    for copy in swaps:
        copy.wait_send()
    relay.wait_send()
    for step, rows in enumerate((rows0, rows1)):

        def drain(source, sem):
            pltpu.make_async_copy(source, source, sem).wait()

        drain(rows.at[pl.ds(0, chips - 1), pl.ds(0, group)], row_send.at[step])
        drain(rows.at[pl.ds(0, chips), pl.ds(0, group)], mate_send.at[step])
        drain(part_out.at[step], part_send.at[step])
        drain(sum_out.at[step, pl.ds(1, chips - 1)], sum_send.at[step])
        local, remote = hand_out(step)
        local.wait()
        remote.wait()


def local(in_flight, arriving, norm_gain, gate_up, w_down, expert_ids, route_weights):
    sections, chips = lax.axis_size("section"), lax.axis_size("expert") // 2
    _, micros, tokens, features = in_flight.shape
    steps = expert_ids.shape[0]
    ff = w_down.shape[2]
    group = 2 * tokens
    half, full = jnp.bfloat16, jnp.float32
    dma = pltpu.SemaphoreType.DMA
    block = (group, features)
    anywhere = pl.BlockSpec(memory_space=pl.ANY)
    return pl.pallas_call(
        functools.partial(relay_kernel, chips, sections),
        out_shape=jax.ShapeDtypeStruct((steps, 1, micros, tokens, features), half),
        in_specs=[anywhere] * 7,
        out_specs=anywhere,
        scratch_shapes=[
            pltpu.VMEM((chips, 2 * group, features + LANES), half),
            pltpu.VMEM((chips, 2 * group, features), half),
            pltpu.VMEM((steps, chips + 1) + block, half),
            pltpu.VMEM((steps, chips) + block, half),
            pltpu.VMEM((steps, chips) + block, half),
            pltpu.VMEM((steps, chips) + block, half),
            pltpu.VMEM((2,) + block, full),
            pltpu.VMEM(block, full),
            pltpu.VMEM((steps,) + block, half),
            pltpu.VMEM(block, half),
            pltpu.VMEM(block, half),
            pltpu.VMEM((steps,) + block, half),
            pltpu.VMEM((2 * group, ff), half),
            pltpu.VMEM((micros, tokens, LANES), half),
            pltpu.VMEM((1, features), full),
            pltpu.VMEM(gate_up.shape[2:], half),
            pltpu.VMEM(w_down.shape[2:], half),
            pltpu.VMEM(expert_ids.shape, jnp.int32),
            pltpu.VMEM(route_weights.shape, full),
            dma((7,)),
            dma((3,)),
            dma((3,)),
            dma((steps,)),
            dma((steps, chips)),
            dma((steps,)),
            dma((steps, chips)),
            dma((steps,)),
            dma((steps, chips + 1)),
            dma((steps,)),
            dma((steps, chips)),
            dma,
            dma,
            dma((steps,)),
            dma((steps,)),
            dma((steps,)),
        ],
        compiler_params=pltpu.CompilerParams(
            collective_id=0, has_side_effects=True, vmem_limit_bytes=56 * 2**20
        ),
        name="relay",
    )(in_flight, arriving, norm_gain, gate_up, w_down, expert_ids, route_weights)


def solution(mesh):
    return jax.shard_map(
        local,
        mesh=mesh,
        in_specs=(
            P("section", None, "expert", None),
            P(None, None, "expert", None),
            P("section", None),
            P("section", "expert", None, None),
            P("section", "expert", None, None),
            P(None, "section", None, "expert", None),
            P(None, "section", None, "expert", None),
        ),
        out_specs=P(None, "section", None, "expert", None),
        check_vma=False,
    )
```

```python
import functools

import jax
import jax.numpy as jnp
from jax import lax
from jax.experimental import pallas as pl
from jax.experimental.pallas import tpu as pltpu
from jax.sharding import PartitionSpec as P

MESH = pl.DeviceIdType.MESH
LANES = 128
CHUNK = 16


def relay_kernel(
    chips,
    sections,
    in_flight,
    arriving,
    norm_gain,
    gate_up,
    w_down,
    expert_ids,
    route_weights,
    out,
    rows0,
    rows1,
    sum_in,
    sum_out,
    part_out,
    part_in,
    own,
    home,
    inflow,
    entering,
    shifted,
    results,
    hidden,
    shares,
    gain,
    up_weights,
    down_weights,
    ids,
    weights,
    load_sems,
    swap_send,
    swap_recv,
    row_send,
    row_recv,
    mate_send,
    mate_recv,
    sum_send,
    sum_recv,
    part_send,
    part_recv,
    shift_send,
    shift_recv,
    out_send,
    out_recv,
    out_sems,
):
    steps, micros, top_count, tokens = expert_ids.shape[0], *expert_ids.shape[2:]
    features = in_flight.shape[-1]
    ff = w_down.shape[2]
    group = 2 * tokens
    tile = min(256, ff)
    experts = 2 * chips
    chunks = [pl.ds(start, CHUNK) for start in range(0, group, CHUNK)]

    me = lax.axis_index("expert")
    section = lax.axis_index("section")
    chip, core = me // 2, lax.rem(me, 2)
    mate = me + 1 - 2 * core
    role = lax.rem(core + chip, 2)

    def on_ring(distance):
        there = lax.rem(chip + distance * (1 - 2 * role) + chips, chips)
        return 2 * there + lax.rem(role + there, 2)

    ahead, behind = on_ring(1), on_ring(-1)
    section_after = lax.rem(section + 1, sections)
    section_before = lax.rem(section + sections - 1, sections)
    mine = pl.ds(pl.multiple_of(core * tokens, tokens), tokens)
    other = pl.ds(pl.multiple_of((1 - core) * tokens, tokens), tokens)

    loads = [
        pltpu.make_async_copy(source, target, load_sems.at[i])
        for i, (source, target) in enumerate(
            (
                (expert_ids, ids),
                (route_weights, weights),
                (norm_gain, gain),
                (in_flight.at[0, role], inflow.at[0, mine]),
                (arriving.at[0, role], entering.at[mine]),
                (gate_up.at[0, 0], up_weights),
                (w_down.at[0, 0], down_weights),
            )
        )
    ]
    for load in loads:
        load.start()

    barrier = pltpu.get_barrier_semaphore()
    for neighbour in (ahead, behind, mate):
        pl.semaphore_signal(barrier, inc=1, device_id={"expert": neighbour}, device_id_type=MESH)
    for neighbour in (section_after, section_before):
        pl.semaphore_signal(barrier, inc=1, device_id={"section": neighbour}, device_id_type=MESH)

    loads[0].wait()
    loads[1].wait()
    line = lax.broadcasted_iota(jnp.int32, (LANES, tokens), 0)
    is_high = lax.rem(line, 2 * experts) < experts
    for micro in range(micros):
        dense = []
        for step in range(steps):
            step_ids, step_weights = ids[step, 0, micro], weights[step, 0, micro]
            total = jnp.zeros((LANES, tokens), jnp.float32)
            for k in range(top_count):
                named = step_ids[k : k + 1] == lax.rem(line, experts)
                total = total + jnp.where(named, step_weights[k : k + 1], 0.0)
            dense.append(total)
        both = jnp.where(line < 2 * experts, dense[0], dense[1])
        high = both.astype(jnp.bfloat16).astype(jnp.float32)
        shares[micro] = jnp.where(is_high, high, both - high).T.astype(jnp.bfloat16)

    pl.semaphore_wait(barrier, 5)

    def swap(index, source, target):
        return pltpu.make_async_remote_copy(
            source, target, swap_send.at[index], swap_recv.at[index], {"expert": mate}, MESH
        )

    swaps = (
        swap(0, in_flight.at[0, 1 - role], inflow.at[0, mine]),
        swap(1, shares.at[1 - role], rows0.at[0, mine, pl.ds(features, LANES)]),
        swap(2, arriving.at[0, 1 - role], entering.at[mine]),
    )
    for copy in swaps:
        copy.start()
    rows0[0, mine, pl.ds(features, LANES)] = shares[role]
    sum_in[:, 1] = jnp.zeros((steps,) + sum_in.shape[2:], sum_in.dtype)

    mate_lane = lax.broadcasted_iota(jnp.int32, (2 * group, LANES), 1)

    def relay_step(step, rows):
        width = rows.shape[-1]

        def pass_on(k, i):
            return pltpu.make_async_remote_copy(
                rows.at[k, chunks[i]],
                rows.at[k + 1, chunks[i]],
                row_send.at[step],
                row_recv.at[step, k + 1, i],
                {"expert": ahead},
                MESH,
            )

        def to_mate(k):
            return pltpu.make_async_remote_copy(
                rows.at[k, pl.ds(0, group)],
                rows.at[k, pl.ds(group, group)],
                mate_send.at[step],
                mate_recv.at[step, k],
                {"expert": mate},
                MESH,
            )

        def part_to_mate(k):
            return pltpu.make_async_remote_copy(
                part_out.at[step, k],
                part_in.at[step, k],
                part_send.at[step],
                part_recv.at[step, k],
                {"expert": mate},
                MESH,
            )

        def sum_on(k, i):
            return pltpu.make_async_remote_copy(
                sum_out.at[step, k, chunks[i]],
                sum_in.at[step, k + 1, chunks[i]],
                sum_send.at[step],
                sum_recv.at[step, k + 1, i],
                {"expert": ahead},
                MESH,
            )

        def forward(k, i):
            pass_on(k - 1, i).wait_recv()

            @pl.when(k < chips - 1)
            def _():
                pass_on(k, i).start()

        def multiply_up(k):
            to_mate(k).wait_recv()
            block = rows[k, :, pl.ds(0, features)]
            for start in range(0, ff, tile):
                gate = jnp.dot(
                    block, up_weights[:, start : start + tile], preferred_element_type=jnp.float32
                )
                lift = jnp.dot(
                    block,
                    up_weights[:, ff + start : ff + start + tile],
                    preferred_element_type=jnp.float32,
                )
                hidden[:, start : start + tile] = (gate / (1.0 + jnp.exp(-gate)) * lift).astype(
                    jnp.bfloat16
                )

        def multiply_down(k):
            slot = lax.rem(k, 2)
            at = step * 2 * experts + me
            picked = (mate_lane == at) | (mate_lane == at + experts)
            share = rows0[k, :, pl.ds(features, LANES)].astype(jnp.float32)
            share = jnp.sum(jnp.where(picked, share, 0.0), axis=1, keepdims=True)
            for start in range(0, features, tile):
                result = jnp.dot(
                    hidden[...],
                    down_weights[:, start : start + tile],
                    preferred_element_type=jnp.float32,
                )
                result = result.astype(jnp.bfloat16).astype(jnp.float32) * share
                own[slot, :, start : start + tile] = result[:group]
                part_out[step, k, :, start : start + tile] = result[group:].astype(jnp.bfloat16)
            part_to_mate(k).start()

        def add(k, i):
            @pl.when(k > 1)
            def _():
                sum_on(k - 1, i).wait_recv()

            rows_now = chunks[i]
            total = own[lax.rem(k, 2), rows_now] + part_in[step, k, rows_now].astype(jnp.float32)
            total = total + sum_in[step, k, rows_now].astype(jnp.float32)
            sum_out[step, k, rows_now] = total.astype(jnp.bfloat16)
            sum_on(k, i).start()

        def turn(k, carry):
            for i in range(len(chunks)):

                @pl.when(k < chips)
                def _():
                    forward(k, i)

                if i < len(chunks) - 1:

                    @pl.when(k > 2)
                    def _():
                        add(k - 2, i + 1)

                    if i == 0:
                        multiply_up(k - 1)
                    elif i == 1:
                        multiply_down(k - 1)
                else:

                    @pl.when(k < chips)
                    def _():
                        to_mate(k).start()

                    part_to_mate(k - 1).wait_recv()

                    @pl.when(k > 1)
                    def _():
                        add(k - 1, 0)

                    @pl.when(k == 1)
                    def _():
                        home[...] = (
                            own[0]
                            + part_in[step, 0].astype(jnp.float32)
                            + inflow[step].astype(jnp.float32)
                        )

            return carry

        for i, rows_now in enumerate(chunks):
            prepare(step, rows, rows_now, i)
            pass_on(0, i).start()
        to_mate(0).start()
        if step == 0:
            loads[5].wait()
            loads[6].wait()
        lax.fori_loop(1, chips + 1, turn, 0)
        for i in range(1, len(chunks)):
            add(chips - 1, i)
        for i, rows_now in enumerate(chunks):
            sum_on(chips - 1, i).wait_recv()
            last = sum_in[step, chips, rows_now].astype(jnp.float32)
            results[step, rows_now] = (home[rows_now] + last).astype(jnp.bfloat16)
            if step + 1 < steps:
                relay(i).start()

    def relay(i):
        return pltpu.make_async_remote_copy(
            results.at[0, chunks[i]],
            shifted.at[chunks[i]],
            shift_send,
            shift_recv.at[i],
            {"section": section_after},
            MESH,
        )

    def prepare(step, rows, rows_now, i):
        if step > 0:
            relay(i).wait_recv()
            inflow[step, rows_now] = jnp.where(section == 0, entering[rows_now], shifted[rows_now])
        wide = inflow[step, rows_now].astype(jnp.float32)
        inverse = lax.rsqrt(jnp.mean(wide * wide, axis=-1, keepdims=True) + 1e-06)
        rows[0, rows_now, pl.ds(0, features)] = (wide * inverse * gain[...]).astype(jnp.bfloat16)

    def hand_out(step):
        local = pltpu.make_async_copy(
            results.at[step, mine], out.at[step, 0, role], out_sems.at[step]
        )
        remote = pltpu.make_async_remote_copy(
            results.at[step, other],
            out.at[step, 0, role],
            out_send.at[step],
            out_recv.at[step],
            {"expert": mate},
            MESH,
        )
        return local, remote

    loads[2].wait()
    loads[3].wait()
    swaps[0].wait_recv()
    swaps[1].wait_recv()
    relay_step(0, rows0)
    for copy in hand_out(0):
        copy.start()
    loads[4].wait()
    swaps[2].wait_recv()
    relay_step(1, rows1)
    for copy in hand_out(1):
        copy.start()

    for copy in swaps:
        copy.wait_send()

    def drain(source, sem):
        pltpu.make_async_copy(source, source, sem).wait()

    drain(results.at[0], shift_send)
    for step, rows in enumerate((rows0, rows1)):
        drain(rows.at[pl.ds(0, chips - 1), pl.ds(0, group)], row_send.at[step])
        drain(rows.at[pl.ds(0, chips), pl.ds(0, group)], mate_send.at[step])
        drain(part_out.at[step], part_send.at[step])
        drain(sum_out.at[step, pl.ds(1, chips - 1)], sum_send.at[step])
        local, remote = hand_out(step)
        local.wait()
        remote.wait()


def local(in_flight, arriving, norm_gain, gate_up, w_down, expert_ids, route_weights):
    sections, chips = lax.axis_size("section"), lax.axis_size("expert") // 2
    _, micros, tokens, features = in_flight.shape
    steps = expert_ids.shape[0]
    ff = w_down.shape[2]
    group = 2 * tokens
    expert_ids, route_weights = expert_ids.swapaxes(3, 4), route_weights.swapaxes(3, 4)
    half, full = jnp.bfloat16, jnp.float32
    dma = pltpu.SemaphoreType.DMA
    block = (group, features)
    anywhere = pl.BlockSpec(memory_space=pl.ANY)
    return pl.pallas_call(
        functools.partial(relay_kernel, chips, sections),
        out_shape=jax.ShapeDtypeStruct((steps, 1, micros, tokens, features), half),
        in_specs=[anywhere] * 7,
        out_specs=anywhere,
        scratch_shapes=[
            pltpu.VMEM((chips, 2 * group, features + LANES), half),
            pltpu.VMEM((chips, 2 * group, features), half),
            pltpu.VMEM((steps, chips + 1) + block, half),
            pltpu.VMEM((steps, chips) + block, half),
            pltpu.VMEM((steps, chips) + block, half),
            pltpu.VMEM((steps, chips) + block, half),
            pltpu.VMEM((2,) + block, full),
            pltpu.VMEM(block, full),
            pltpu.VMEM((steps,) + block, half),
            pltpu.VMEM(block, half),
            pltpu.VMEM(block, half),
            pltpu.VMEM((steps,) + block, half),
            pltpu.VMEM((2 * group, ff), half),
            pltpu.VMEM((micros, tokens, LANES), half),
            pltpu.VMEM((1, features), full),
            pltpu.VMEM(gate_up.shape[2:], half),
            pltpu.VMEM(w_down.shape[2:], half),
            pltpu.VMEM(expert_ids.shape, jnp.int32),
            pltpu.VMEM(route_weights.shape, full),
            dma((7,)),
            dma((3,)),
            dma((3,)),
            dma((steps,)),
            dma((steps, chips, group // CHUNK)),
            dma((steps,)),
            dma((steps, chips)),
            dma((steps,)),
            dma((steps, chips + 1, group // CHUNK)),
            dma((steps,)),
            dma((steps, chips)),
            dma,
            dma((group // CHUNK,)),
            dma((steps,)),
            dma((steps,)),
            dma((steps,)),
        ],
        compiler_params=pltpu.CompilerParams(
            collective_id=0, has_side_effects=True, vmem_limit_bytes=56 * 2**20
        ),
        name="relay",
    )(in_flight, arriving, norm_gain, gate_up, w_down, expert_ids, route_weights)


def solution(mesh):
    return jax.shard_map(
        local,
        mesh=mesh,
        in_specs=(
            P("section", None, "expert", None),
            P(None, None, "expert", None),
            P("section", None),
            P("section", "expert", None, None),
            P("section", "expert", None, None),
            P(None, "section", None, "expert", None),
            P(None, "section", None, "expert", None),
        ),
        out_specs=P(None, "section", None, "expert", None),
        check_vma=False,
    )
```

```python
import functools

import jax
import jax.numpy as jnp
from jax import lax
from jax.experimental import pallas as pl
from jax.experimental.pallas import tpu as pltpu
from jax.sharding import PartitionSpec as P

MESH = pl.DeviceIdType.MESH
LANES = 128
CHUNK = 16


def relay_kernel(
    chips,
    sections,
    in_flight,
    arriving,
    norm_gain,
    gate_up,
    w_down,
    expert_ids,
    route_weights,
    out,
    rows0,
    rows1,
    sum_in,
    sum_out,
    part_out,
    part_in,
    own,
    home,
    home_before,
    home_mate,
    inflow,
    entering,
    sum_before,
    sum_last,
    first,
    last,
    hidden,
    shares,
    gain,
    up_weights,
    down_weights,
    ids,
    weights,
    load_sems,
    swap_send,
    swap_recv,
    row_send,
    row_recv,
    mate_send,
    mate_recv,
    sum_send,
    sum_recv,
    part_send,
    part_recv,
    home_send,
    home_recv,
    before_send,
    before_recv,
    last_send,
    last_recv,
    out_send,
    out_recv,
    out_sems,
):
    steps, micros, top_count, tokens = expert_ids.shape[0], *expert_ids.shape[2:]
    features = in_flight.shape[-1]
    ff = w_down.shape[2]
    group = 2 * tokens
    tile = min(256, ff)
    experts = 2 * chips
    mine, other, block = pl.ds(0, tokens), pl.ds(tokens, tokens), pl.ds(0, group)
    chunks = [pl.ds(start, CHUNK) for start in range(0, group, CHUNK)]
    half = len(chunks) // 2

    me = lax.axis_index("expert")
    section = lax.axis_index("section")
    chip, core = me // 2, lax.rem(me, 2)
    mate = me + 1 - 2 * core
    role = lax.rem(core + chip, 2)

    def on_ring(distance):
        there = lax.rem(chip + distance * (1 - 2 * role) + chips, chips)
        return 2 * there + lax.rem(role + there, 2)

    ahead, behind = on_ring(1), on_ring(-1)
    ahead_mate = ahead + 1 - 2 * lax.rem(ahead, 2)
    has_after, has_before = section < sections - 1, section > 0
    section_after, section_before = section + 1, section - 1

    barrier = pltpu.get_barrier_semaphore()

    def greet(where):
        pl.semaphore_signal(barrier, inc=1, device_id=where, device_id_type=MESH)

    for device in (mate, behind, ahead_mate):
        greet({"expert": device})

    @pl.when(has_before)
    def _():
        greet({"section": section_before})
        greet({"section": section_before, "expert": behind})

    loads = [
        pltpu.make_async_copy(source, target, load_sems.at[i])
        for i, (source, target) in enumerate(
            (
                (in_flight.at[0, role], inflow.at[0, mine]),
                (norm_gain, gain),
                (expert_ids, ids),
                (route_weights, weights),
                (arriving.at[0, role], entering.at[mine]),
                (gate_up.at[0, 0], up_weights),
                (w_down.at[0, 0], down_weights),
            )
        )
    ]
    for load in loads:
        load.start()

    def normalize(step, rows, rows_now):
        wide = inflow[step, rows_now].astype(jnp.float32)
        inverse = lax.rsqrt(jnp.mean(wide * wide, axis=-1, keepdims=True) + 1e-06)
        rows[0, rows_now, pl.ds(0, features)] = (wide * inverse * gain[...]).astype(jnp.bfloat16)

    loads[0].wait()
    loads[1].wait()
    normalize(0, rows0, mine)

    loads[2].wait()
    loads[3].wait()
    line = lax.broadcasted_iota(jnp.int32, (LANES, tokens), 0)
    is_high = lax.rem(line, 2 * experts) < experts
    for micro in range(micros):
        dense = []
        for step in range(steps):
            step_ids, step_weights = ids[step, 0, micro], weights[step, 0, micro]
            total = jnp.zeros((LANES, tokens), jnp.float32)
            for k in range(top_count):
                named = step_ids[k : k + 1] == lax.rem(line, experts)
                total = total + jnp.where(named, step_weights[k : k + 1], 0.0)
            dense.append(total)
        both = jnp.where(line < 2 * experts, dense[0], dense[1])
        high = both.astype(jnp.bfloat16).astype(jnp.float32)
        shares[micro] = jnp.where(is_high, high, both - high).T.astype(jnp.bfloat16)
    rows0[0, mine, pl.ds(features, LANES)] = shares[role]

    pl.semaphore_wait(barrier, 3 + 2 * has_after.astype(jnp.int32))

    def swap(index, source, target):
        return pltpu.make_async_remote_copy(
            source, target, swap_send.at[index], swap_recv.at[index], {"expert": mate}, MESH
        )

    swaps = (
        swap(0, in_flight.at[0, 1 - role], inflow.at[0, other]),
        swap(1, shares.at[1 - role], rows0.at[0, other, pl.ds(features, LANES)]),
        swap(2, arriving.at[0, 1 - role], entering.at[other]),
    )
    swaps[0].start()
    swaps[1].start()

    mate_lane = lax.broadcasted_iota(jnp.int32, (2 * group, LANES), 1)

    home_on = pltpu.make_async_remote_copy(
        home.at[0], home_before, home_send.at[0], home_recv.at[0], {"section": section_after}, MESH
    )
    home_over = pltpu.make_async_remote_copy(
        home.at[1, other], home_mate, home_send.at[1], home_recv.at[1], {"expert": mate}, MESH
    )

    def sum_to_next_section(i):
        return pltpu.make_async_remote_copy(
            sum_out.at[0, chips - 1, chunks[i]],
            sum_before.at[chunks[i]],
            before_send,
            before_recv.at[i],
            {"section": section_after, "expert": ahead},
            MESH,
        )

    def sum_to_owner(i, micro=role):
        return pltpu.make_async_remote_copy(
            sum_out.at[1, chips - 1, chunks[i]],
            sum_last.at[micro, chunks[i % half]],
            last_send,
            last_recv.at[micro, i % half],
            {"expert": ahead if i < half else ahead_mate},
            MESH,
        )

    def relay_step(step, rows):
        def pass_on(k, i):
            return pltpu.make_async_remote_copy(
                rows.at[k, chunks[i]],
                rows.at[k + 1, chunks[i]],
                row_send.at[step],
                row_recv.at[step, k + 1, i],
                {"expert": ahead},
                MESH,
            )

        def to_mate(k, i):
            return pltpu.make_async_remote_copy(
                rows.at[k, chunks[i]],
                rows.at[k, pl.ds(group + i * CHUNK, CHUNK)],
                mate_send.at[step],
                mate_recv.at[step, k],
                {"expert": mate},
                MESH,
            )

        def part_to_mate(k):
            return pltpu.make_async_remote_copy(
                part_out.at[step, k],
                part_in.at[step, k],
                part_send.at[step],
                part_recv.at[step, k],
                {"expert": mate},
                MESH,
            )

        def sum_on(k, i):
            return pltpu.make_async_remote_copy(
                sum_out.at[step, k, chunks[i]],
                sum_in.at[step, k + 1, chunks[i]],
                sum_send.at[step],
                sum_recv.at[step, k + 1, i],
                {"expert": ahead},
                MESH,
            )

        def forward(k, i):
            pass_on(k - 1, i).wait_recv()

            @pl.when(k < chips - 1)
            def _():
                pass_on(k, i).start()

            to_mate(k, i).start()

        def multiply_up(k):
            arrived = rows.at[k, pl.ds(group, group)]
            pltpu.make_async_copy(arrived, arrived, mate_recv.at[step, k]).wait()
            both = rows[k, :, pl.ds(0, features)]
            for start in range(0, ff, tile):
                gate = jnp.dot(
                    both, up_weights[:, start : start + tile], preferred_element_type=jnp.float32
                )
                lift = jnp.dot(
                    both,
                    up_weights[:, ff + start : ff + start + tile],
                    preferred_element_type=jnp.float32,
                )
                hidden[:, start : start + tile] = (gate / (1.0 + jnp.exp(-gate)) * lift).astype(
                    jnp.bfloat16
                )

        def multiply_down(k):
            slot = lax.rem(k, 2)
            at = step * 2 * experts + me
            picked = (mate_lane == at) | (mate_lane == at + experts)
            share = rows0[k, :, pl.ds(features, LANES)].astype(jnp.float32)
            share = jnp.sum(jnp.where(picked, share, 0.0), axis=1, keepdims=True)
            for start in range(0, features, tile):
                result = jnp.dot(
                    hidden[...],
                    down_weights[:, start : start + tile],
                    preferred_element_type=jnp.float32,
                )
                result = result.astype(jnp.bfloat16).astype(jnp.float32) * share
                own[slot, :, start : start + tile] = result[:group]
                part_out[step, k, :, start : start + tile] = result[group:].astype(jnp.bfloat16)
            part_to_mate(k).start()

        def add(k, i):
            @pl.when(k > 1)
            def _():
                sum_on(k - 1, i).wait_recv()

            rows_now = chunks[i]
            total = own[lax.rem(k, 2), rows_now] + part_in[step, k, rows_now].astype(jnp.float32)
            total = total + sum_in[step, k, rows_now].astype(jnp.float32)
            sum_out[step, k, rows_now] = total.astype(jnp.bfloat16)

        def add_on(k, i):
            add(k, i)
            sum_on(k, i).start()

        def turn(k, carry):
            for i in range(len(chunks)):

                @pl.when(k < chips)
                def _():
                    forward(k, i)

                if i < len(chunks) - 1:

                    @pl.when(k > 2)
                    def _():
                        add_on(k - 2, i + 1)

                    if i == 0:
                        multiply_up(k - 1)
                    elif i == 1:
                        multiply_down(k - 1)
                else:
                    part_to_mate(k - 1).wait_recv()

                    @pl.when((k > 1) & (k < chips))
                    def _():
                        add_on(k - 1, 0)

                    @pl.when(k == 1)
                    def _():
                        home[step] = (
                            own[0]
                            + part_in[step, 0].astype(jnp.float32)
                            + inflow[step].astype(jnp.float32)
                        )
                        if step == 0:

                            @pl.when(has_after)
                            def _():
                                home_on.start()

                        else:
                            home_over.start()

            return carry

        for i, rows_now in enumerate(chunks):
            if step == 0 and i == half:
                swaps[0].wait_recv()
                swaps[1].wait_recv()
                normalize(0, rows, other)
            if step == 1:
                if i == 0:

                    @pl.when(has_before)
                    def _():
                        home_on.wait_recv()

                @pl.when(has_before)
                def _():
                    sum_to_next_section(i).wait_recv()
                    total = home_before[rows_now] + sum_before[rows_now].astype(jnp.float32)
                    inflow[1, rows_now] = total.astype(jnp.bfloat16)

                @pl.when(section == 0)
                def _():
                    inflow[1, rows_now] = entering[rows_now]

                normalize(1, rows, rows_now)
            pass_on(0, i).start()
            to_mate(0, i).start()
        if step == 0:
            swaps[2].start()
            sum_in[:, 1] = jnp.zeros((steps,) + sum_in.shape[2:], sum_in.dtype)
            loads[5].wait()
            loads[6].wait()
        lax.fori_loop(1, chips + 1, turn, 0)
        for i in range(len(chunks)):
            add(chips - 1, i)
            if step == 0:

                @pl.when(has_after)
                def _():
                    sum_to_next_section(i).start()

                sum_on(chips - 1, i).start()
            else:
                sum_to_owner(i).start()
        if step == 0:
            loads[4].wait()
            swaps[2].wait_recv()

    relay_step(0, rows0)

    def first_out():
        return (
            pltpu.make_async_copy(first.at[mine], out.at[0, 0, role], out_sems.at[0]),
            pltpu.make_async_remote_copy(
                first.at[other], out.at[0, 0, role], out_send, out_recv, {"expert": mate}, MESH
            ),
        )

    relay_step(1, rows1)

    for i, rows_now in enumerate(chunks):
        come_round = sum_in.at[0, chips, rows_now]
        pltpu.make_async_copy(come_round, come_round, sum_recv.at[0, chips, i]).wait()
        first[rows_now] = (home[0, rows_now] + come_round[...].astype(jnp.float32)).astype(
            jnp.bfloat16
        )
    for copy in first_out():
        copy.start()

    home_over.wait_recv()
    for i in range(half):
        sum_to_owner(i).wait_recv()
        total = home[1, chunks[i]] + sum_last[role, chunks[i]].astype(jnp.float32)
        last[role, chunks[i]] = total.astype(jnp.bfloat16)
    for i in range(half):
        sum_to_owner(i, 1 - role).wait_recv()
        total = home_mate[chunks[i]] + sum_last[1 - role, chunks[i]].astype(jnp.float32)
        last[1 - role, chunks[i]] = total.astype(jnp.bfloat16)
    last_out = pltpu.make_async_copy(last, out.at[1, 0], out_sems.at[1])
    last_out.start()

    def drain(source, sem):
        pltpu.make_async_copy(source, source, sem).wait()

    for copy in swaps:
        copy.wait_send()

    @pl.when(has_after)
    def _():
        home_on.wait_send()
        drain(sum_out.at[0, chips - 1], before_send)

    home_over.wait_send()
    drain(sum_out.at[1, chips - 1], last_send)
    for step, rows in enumerate((rows0, rows1)):
        drain(rows.at[pl.ds(0, chips - 1), block], row_send.at[step])
        drain(rows.at[pl.ds(0, chips), block], mate_send.at[step])
        drain(part_out.at[step], part_send.at[step])
        sums = pl.ds(1, chips - 1 - step)
        drain(sum_out.at[step, sums], sum_send.at[step])
    for copy in first_out():
        copy.wait()
    last_out.wait()


def local(in_flight, arriving, norm_gain, gate_up, w_down, expert_ids, route_weights):
    sections, chips = lax.axis_size("section"), lax.axis_size("expert") // 2
    _, micros, tokens, features = in_flight.shape
    steps = expert_ids.shape[0]
    ff = w_down.shape[2]
    group = 2 * tokens
    pieces = group // CHUNK
    expert_ids, route_weights = expert_ids.swapaxes(3, 4), route_weights.swapaxes(3, 4)
    half, full = jnp.bfloat16, jnp.float32
    dma = pltpu.SemaphoreType.DMA
    block = (group, features)
    anywhere = pl.BlockSpec(memory_space=pl.ANY)
    return pl.pallas_call(
        functools.partial(relay_kernel, chips, sections),
        out_shape=jax.ShapeDtypeStruct((steps, 1, micros, tokens, features), half),
        in_specs=[anywhere] * 7,
        out_specs=anywhere,
        scratch_shapes=[
            pltpu.VMEM((chips, 2 * group, features + LANES), half),
            pltpu.VMEM((chips, 2 * group, features), half),
            pltpu.VMEM((steps, chips + 1) + block, half),
            pltpu.VMEM((steps, chips) + block, half),
            pltpu.VMEM((steps, chips) + block, half),
            pltpu.VMEM((steps, chips) + block, half),
            pltpu.VMEM((2,) + block, full),
            pltpu.VMEM((steps,) + block, full),
            pltpu.VMEM(block, full),
            pltpu.VMEM((tokens, features), full),
            pltpu.VMEM((steps,) + block, half),
            pltpu.VMEM(block, half),
            pltpu.VMEM(block, half),
            pltpu.VMEM((micros, tokens, features), half),
            pltpu.VMEM(block, half),
            pltpu.VMEM((micros, tokens, features), half),
            pltpu.VMEM((2 * group, ff), half),
            pltpu.VMEM((micros, tokens, LANES), half),
            pltpu.VMEM((1, features), full),
            pltpu.VMEM(gate_up.shape[2:], half),
            pltpu.VMEM(w_down.shape[2:], half),
            pltpu.VMEM(expert_ids.shape, jnp.int32),
            pltpu.VMEM(route_weights.shape, full),
            dma((7,)),
            dma((3,)),
            dma((3,)),
            dma((steps,)),
            dma((steps, chips, pieces)),
            dma((steps,)),
            dma((steps, chips)),
            dma((steps,)),
            dma((steps, chips + 1, pieces)),
            dma((steps,)),
            dma((steps, chips)),
            dma((2,)),
            dma((2,)),
            dma,
            dma((pieces,)),
            dma,
            dma((micros, pieces // 2)),
            dma,
            dma,
            dma((steps,)),
        ],
        compiler_params=pltpu.CompilerParams(
            collective_id=0, has_side_effects=True, vmem_limit_bytes=56 * 2**20
        ),
        name="relay",
    )(in_flight, arriving, norm_gain, gate_up, w_down, expert_ids, route_weights)


def solution(mesh):
    return jax.shard_map(
        local,
        mesh=mesh,
        in_specs=(
            P("section", None, "expert", None),
            P(None, None, "expert", None),
            P("section", None),
            P("section", "expert", None, None),
            P("section", "expert", None, None),
            P(None, "section", None, "expert", None),
            P(None, "section", None, "expert", None),
        ),
        out_specs=P(None, "section", None, "expert", None),
        check_vma=False,
    )
```

```python
import functools

import jax
import jax.numpy as jnp
from jax import lax
from jax.experimental import pallas as pl
from jax.experimental.pallas import tpu as pltpu
from jax.sharding import PartitionSpec as P

MESH = pl.DeviceIdType.MESH
LANES = 128
CHUNK = 16
TURN = (
    ("row", 0, 0),
    ("sum", 2, 3),
    ("down", 1, 0),
    ("row", 0, 1),
    ("row", 0, 2),
    ("row", 0, 3),
    ("part", 1, 0),
    ("sum", 1, 0),
    ("sum", 1, 1),
    ("sum", 1, 2),
    ("up", 0, 0),
)


def when(condition):
    if isinstance(condition, bool):
        return (lambda work: work()) if condition else (lambda work: None)
    return pl.when(condition)


def relay_kernel(
    chips,
    sections,
    in_flight,
    arriving,
    norm_gain,
    gate_up,
    w_down,
    expert_ids,
    route_weights,
    out,
    rows0,
    rows1,
    sum_in,
    sum_out,
    part_out,
    part_in,
    own,
    home,
    home_before,
    home_mate,
    inflow,
    entering,
    sum_before,
    sum_last,
    first,
    last,
    hidden,
    shares,
    gain,
    up_weights,
    down_weights,
    ids,
    weights,
    load_sems,
    swap_send,
    swap_recv,
    row_send,
    row_recv,
    mate_send,
    mate_recv,
    sum_send,
    sum_recv,
    part_send,
    part_recv,
    home_send,
    home_recv,
    before_send,
    before_recv,
    last_send,
    last_recv,
    out_send,
    out_recv,
    out_sems,
):
    steps, micros, top_count, tokens = expert_ids.shape[0], *expert_ids.shape[2:]
    features = in_flight.shape[-1]
    ff = w_down.shape[2]
    group = 2 * tokens
    tile = min(256, ff)
    experts = 2 * chips
    mine, other, block = pl.ds(0, tokens), pl.ds(tokens, tokens), pl.ds(0, group)
    chunks = [pl.ds(start, CHUNK) for start in range(0, group, CHUNK)]
    half = len(chunks) // 2

    me = lax.axis_index("expert")
    section = lax.axis_index("section")
    chip, core = me // 2, lax.rem(me, 2)
    mate = me + 1 - 2 * core
    role = lax.rem(core + chip, 2)

    def on_ring(distance):
        there = lax.rem(chip + distance * (1 - 2 * role) + chips, chips)
        return 2 * there + lax.rem(role + there, 2)

    ahead, behind = on_ring(1), on_ring(-1)
    ahead_mate = ahead + 1 - 2 * lax.rem(ahead, 2)
    has_after, has_before = section < sections - 1, section > 0
    section_after, section_before = section + 1, section - 1

    barrier = pltpu.get_barrier_semaphore()

    def greet(where):
        pl.semaphore_signal(barrier, inc=1, device_id=where, device_id_type=MESH)

    for device in (mate, behind, ahead_mate):
        greet({"expert": device})

    @pl.when(has_before)
    def _():
        greet({"section": section_before})
        greet({"section": section_before, "expert": behind})

    loads = [
        pltpu.make_async_copy(source, target, load_sems.at[i])
        for i, (source, target) in enumerate(
            (
                (in_flight.at[0, role], inflow.at[0, mine]),
                (norm_gain, gain),
                (expert_ids, ids),
                (route_weights, weights),
                (arriving.at[0, role], entering.at[mine]),
                (gate_up.at[0, 0], up_weights),
                (w_down.at[0, 0], down_weights),
            )
        )
    ]
    for load in loads:
        load.start()

    def normalize(step, rows, rows_now):
        wide = inflow[step, rows_now].astype(jnp.float32)
        inverse = lax.rsqrt(jnp.mean(wide * wide, axis=-1, keepdims=True) + 1e-06)
        rows[0, rows_now, pl.ds(0, features)] = (wide * inverse * gain[...]).astype(jnp.bfloat16)

    pl.semaphore_wait(barrier, 3 + 2 * has_after.astype(jnp.int32))

    def swap(index, source, target):
        return pltpu.make_async_remote_copy(
            source, target, swap_send.at[index], swap_recv.at[index], {"expert": mate}, MESH
        )

    swaps = (
        swap(0, in_flight.at[0, 1 - role], inflow.at[0, other]),
        swap(1, shares.at[1 - role], rows0.at[0, other, pl.ds(features, LANES)]),
        swap(2, arriving.at[0, 1 - role], entering.at[other]),
    )
    swaps[0].start()

    loads[2].wait()
    loads[3].wait()
    line = lax.broadcasted_iota(jnp.int32, (LANES, tokens), 0)
    is_high = lax.rem(line, 2 * experts) < experts
    for micro in range(micros):
        dense = []
        for step in range(steps):
            step_ids, step_weights = ids[step, 0, micro], weights[step, 0, micro]
            total = jnp.zeros((LANES, tokens), jnp.float32)
            for k in range(top_count):
                named = step_ids[k : k + 1] == lax.rem(line, experts)
                total = total + jnp.where(named, step_weights[k : k + 1], 0.0)
            dense.append(total)
        both = jnp.where(line < 2 * experts, dense[0], dense[1])
        high = both.astype(jnp.bfloat16).astype(jnp.float32)
        shares[micro] = jnp.where(is_high, high, both - high).T.astype(jnp.bfloat16)
    swaps[1].start()
    rows0[0, mine, pl.ds(features, LANES)] = shares[role]

    loads[0].wait()
    loads[1].wait()
    normalize(0, rows0, mine)

    mate_lane = lax.broadcasted_iota(jnp.int32, (2 * group, LANES), 1)

    home_on = pltpu.make_async_remote_copy(
        home.at[0], home_before, home_send.at[0], home_recv.at[0], {"section": section_after}, MESH
    )
    home_over = pltpu.make_async_remote_copy(
        home.at[1, other], home_mate, home_send.at[1], home_recv.at[1], {"expert": mate}, MESH
    )

    def sum_to_next_section(i):
        return pltpu.make_async_remote_copy(
            sum_out.at[0, chips - 1, chunks[i]],
            sum_before.at[chunks[i]],
            before_send,
            before_recv.at[i],
            {"section": section_after, "expert": ahead},
            MESH,
        )

    def sum_to_owner(i, micro=role):
        return pltpu.make_async_remote_copy(
            sum_out.at[1, chips - 1, chunks[i]],
            sum_last.at[micro, chunks[i % half]],
            last_send,
            last_recv.at[micro, i % half],
            {"expert": ahead if i < half else ahead_mate},
            MESH,
        )

    def relay_step(step, rows):
        def pass_on(k, i):
            return pltpu.make_async_remote_copy(
                rows.at[k, chunks[i]],
                rows.at[k + 1, chunks[i]],
                row_send.at[step],
                row_recv.at[step, k + 1, i],
                {"expert": ahead},
                MESH,
            )

        def to_mate(k, i):
            return pltpu.make_async_remote_copy(
                rows.at[k, chunks[i]],
                rows.at[k, pl.ds(group + i * CHUNK, CHUNK)],
                mate_send.at[step],
                mate_recv.at[step, k],
                {"expert": mate},
                MESH,
            )

        def part_to_mate(k):
            return pltpu.make_async_remote_copy(
                part_out.at[step, k],
                part_in.at[step, k],
                part_send.at[step],
                part_recv.at[step, k],
                {"expert": mate},
                MESH,
            )

        def sum_on(k, i):
            return pltpu.make_async_remote_copy(
                sum_out.at[step, k, chunks[i]],
                sum_in.at[step, k + 1, chunks[i]],
                sum_send.at[step],
                sum_recv.at[step, k + 1, i],
                {"expert": ahead},
                MESH,
            )

        def forward(k, i):
            pass_on(k - 1, i).wait_recv()

            @pl.when(k < chips - 1)
            def _():
                pass_on(k, i).start()

            to_mate(k, i).start()

        def multiply_up(k):
            arrived = rows.at[k, pl.ds(group, group)]
            pltpu.make_async_copy(arrived, arrived, mate_recv.at[step, k]).wait()
            both = rows[k, :, pl.ds(0, features)]
            for start in range(0, ff, tile):
                gate = jnp.dot(
                    both, up_weights[:, start : start + tile], preferred_element_type=jnp.float32
                )
                lift = jnp.dot(
                    both,
                    up_weights[:, ff + start : ff + start + tile],
                    preferred_element_type=jnp.float32,
                )
                hidden[:, start : start + tile] = (gate / (1.0 + jnp.exp(-gate)) * lift).astype(
                    jnp.bfloat16
                )

        def multiply_down(k):
            slot = lax.rem(k, 2)
            at = step * 2 * experts + me
            picked = (mate_lane == at) | (mate_lane == at + experts)
            share = rows0[k, :, pl.ds(features, LANES)].astype(jnp.float32)
            share = jnp.sum(jnp.where(picked, share, 0.0), axis=1, keepdims=True)
            for start in range(0, features, tile):
                result = jnp.dot(
                    hidden[...],
                    down_weights[:, start : start + tile],
                    preferred_element_type=jnp.float32,
                )
                result = result.astype(jnp.bfloat16).astype(jnp.float32) * share
                own[slot, :, start : start + tile] = result[:group]
                part_out[step, k, :, start : start + tile] = result[group:].astype(jnp.bfloat16)
            part_to_mate(k).start()

        def add(k, i):
            @pl.when(k > 1)
            def _():
                sum_on(k - 1, i).wait_recv()

            rows_now = chunks[i]
            total = own[lax.rem(k, 2), rows_now] + part_in[step, k, rows_now].astype(jnp.float32)
            total = total + sum_in[step, k, rows_now].astype(jnp.float32)
            sum_out[step, k, rows_now] = total.astype(jnp.bfloat16)

        def add_on(k, i):
            add(k, i)
            sum_on(k, i).start()

        def take_part(k):
            part_to_mate(k).wait_recv()

            @when(k == 0)
            def _():
                home[step] = (
                    own[0]
                    + part_in[step, 0].astype(jnp.float32)
                    + inflow[step].astype(jnp.float32)
                )
                if step == 0:

                    @pl.when(has_after)
                    def _():
                        home_on.start()

                else:
                    home_over.start()

        def finish(i):
            add(chips - 1, i)
            if step == 0:

                @pl.when(has_after)
                def _():
                    sum_to_next_section(i).start()

            else:
                sum_to_owner(i).start()

        def turn(k):
            for what, behind_by, i in TURN:
                b = k - behind_by
                if isinstance(b, int) and not 0 <= b < chips:
                    continue
                if what == "row":
                    if not isinstance(b, int) or b > 0:
                        forward(b, i)
                elif what == "up":
                    when(b >= 0)(functools.partial(multiply_up, b))
                elif what == "down":
                    when(b >= 0)(functools.partial(multiply_down, b))
                elif what == "part":
                    when(b >= 0)(functools.partial(take_part, b))
                elif isinstance(b, int) and b == chips - 1:
                    finish(i)
                else:
                    when(b > 0)(functools.partial(add_on, b, i))

        for i, rows_now in enumerate(chunks):
            if step == 0 and i == half:
                swaps[0].wait_recv()
                swaps[1].wait_recv()
                normalize(0, rows, other)
            if step == 1:
                if i == 0:

                    @pl.when(has_before)
                    def _():
                        home_on.wait_recv()

                @pl.when(has_before)
                def _():
                    sum_to_next_section(i).wait_recv()
                    total = home_before[rows_now] + sum_before[rows_now].astype(jnp.float32)
                    inflow[1, rows_now] = total.astype(jnp.bfloat16)

                @pl.when(section == 0)
                def _():
                    inflow[1, rows_now] = entering[rows_now]

                normalize(1, rows, rows_now)
            pass_on(0, i).start()
            to_mate(0, i).start()
        if step == 0:
            swaps[2].start()
            sum_in[:, 1] = jnp.zeros((steps,) + sum_in.shape[2:], sum_in.dtype)
            loads[5].wait()
            loads[6].wait()
        turn(0)
        pl.loop(1, chips)(turn)
        for k in range(chips, chips + 1 + max(behind_by for _, behind_by, _ in TURN)):
            turn(k)
        if step == 0:
            for i in range(len(chunks)):
                sum_on(chips - 1, i).start()
            loads[4].wait()
            swaps[2].wait_recv()

    relay_step(0, rows0)

    def first_out():
        return (
            pltpu.make_async_copy(first.at[mine], out.at[0, 0, role], out_sems.at[0]),
            pltpu.make_async_remote_copy(
                first.at[other], out.at[0, 0, role], out_send, out_recv, {"expert": mate}, MESH
            ),
        )

    relay_step(1, rows1)

    for i, rows_now in enumerate(chunks):
        come_round = sum_in.at[0, chips, rows_now]
        pltpu.make_async_copy(come_round, come_round, sum_recv.at[0, chips, i]).wait()
        first[rows_now] = (home[0, rows_now] + come_round[...].astype(jnp.float32)).astype(
            jnp.bfloat16
        )
    for copy in first_out():
        copy.start()

    home_over.wait_recv()
    for i in range(half):
        sum_to_owner(i).wait_recv()
        total = home[1, chunks[i]] + sum_last[role, chunks[i]].astype(jnp.float32)
        last[role, chunks[i]] = total.astype(jnp.bfloat16)
    for i in range(half):
        sum_to_owner(i, 1 - role).wait_recv()
        total = home_mate[chunks[i]] + sum_last[1 - role, chunks[i]].astype(jnp.float32)
        last[1 - role, chunks[i]] = total.astype(jnp.bfloat16)
    last_out = pltpu.make_async_copy(last, out.at[1, 0], out_sems.at[1])
    last_out.start()

    def drain(source, sem):
        pltpu.make_async_copy(source, source, sem).wait()

    for copy in swaps:
        copy.wait_send()

    @pl.when(has_after)
    def _():
        home_on.wait_send()
        drain(sum_out.at[0, chips - 1], before_send)

    home_over.wait_send()
    drain(sum_out.at[1, chips - 1], last_send)
    for step, rows in enumerate((rows0, rows1)):
        drain(rows.at[pl.ds(0, chips - 1), block], row_send.at[step])
        drain(rows.at[pl.ds(0, chips), block], mate_send.at[step])
        drain(part_out.at[step], part_send.at[step])
        sums = pl.ds(1, chips - 1 - step)
        drain(sum_out.at[step, sums], sum_send.at[step])
    for copy in first_out():
        copy.wait()
    last_out.wait()


def local(in_flight, arriving, norm_gain, gate_up, w_down, expert_ids, route_weights):
    sections, chips = lax.axis_size("section"), lax.axis_size("expert") // 2
    _, micros, tokens, features = in_flight.shape
    steps = expert_ids.shape[0]
    ff = w_down.shape[2]
    group = 2 * tokens
    pieces = group // CHUNK
    expert_ids, route_weights = expert_ids.swapaxes(3, 4), route_weights.swapaxes(3, 4)
    half, full = jnp.bfloat16, jnp.float32
    dma = pltpu.SemaphoreType.DMA
    block = (group, features)
    anywhere = pl.BlockSpec(memory_space=pl.ANY)
    return pl.pallas_call(
        functools.partial(relay_kernel, chips, sections),
        out_shape=pltpu.VMEM((steps, 1, micros, tokens, features), half),
        in_specs=[anywhere] * 7,
        out_specs=pl.BlockSpec(memory_space=pltpu.VMEM),
        scratch_shapes=[
            pltpu.VMEM((chips, 2 * group, features + LANES), half),
            pltpu.VMEM((chips, 2 * group, features), half),
            pltpu.VMEM((steps, chips + 1) + block, half),
            pltpu.VMEM((steps, chips) + block, half),
            pltpu.VMEM((steps, chips) + block, half),
            pltpu.VMEM((steps, chips) + block, half),
            pltpu.VMEM((2,) + block, full),
            pltpu.VMEM((steps,) + block, full),
            pltpu.VMEM(block, full),
            pltpu.VMEM((tokens, features), full),
            pltpu.VMEM((steps,) + block, half),
            pltpu.VMEM(block, half),
            pltpu.VMEM(block, half),
            pltpu.VMEM((micros, tokens, features), half),
            pltpu.VMEM(block, half),
            pltpu.VMEM((micros, tokens, features), half),
            pltpu.VMEM((2 * group, ff), half),
            pltpu.VMEM((micros, tokens, LANES), half),
            pltpu.VMEM((1, features), full),
            pltpu.VMEM(gate_up.shape[2:], half),
            pltpu.VMEM(w_down.shape[2:], half),
            pltpu.VMEM(expert_ids.shape, jnp.int32),
            pltpu.VMEM(route_weights.shape, full),
            dma((7,)),
            dma((3,)),
            dma((3,)),
            dma((steps,)),
            dma((steps, chips, pieces)),
            dma((steps,)),
            dma((steps, chips)),
            dma((steps,)),
            dma((steps, chips + 1, pieces)),
            dma((steps,)),
            dma((steps, chips)),
            dma((2,)),
            dma((2,)),
            dma,
            dma((pieces,)),
            dma,
            dma((micros, pieces // 2)),
            dma,
            dma,
            dma((steps,)),
        ],
        compiler_params=pltpu.CompilerParams(
            collective_id=0, has_side_effects=True, vmem_limit_bytes=56 * 2**20
        ),
        name="relay",
    )(in_flight, arriving, norm_gain, gate_up, w_down, expert_ids, route_weights)


def solution(mesh):
    return jax.shard_map(
        local,
        mesh=mesh,
        in_specs=(
            P("section", None, "expert", None),
            P(None, None, "expert", None),
            P("section", None),
            P("section", "expert", None, None),
            P("section", "expert", None, None),
            P(None, "section", None, "expert", None),
            P(None, "section", None, "expert", None),
        ),
        out_specs=P(None, "section", None, "expert", None),
        check_vma=False,
    )
```

```python
import functools

import jax
import jax.numpy as jnp
from jax import lax
from jax.experimental import pallas as pl
from jax.experimental.pallas import tpu as pltpu
from jax.sharding import PartitionSpec as P

MESH = pl.DeviceIdType.MESH
LANES = 128
CHUNK = 16
TURN = (
    ("row", 0, 0),
    ("sum", 2, 3),
    ("down", 1, 0),
    ("row", 0, 1),
    ("row", 0, 2),
    ("row", 0, 3),
    ("part", 1, 0),
    ("sum", 1, 0),
    ("sum", 1, 1),
    ("sum", 1, 2),
    ("up", 0, 0),
)


def when(condition):
    if isinstance(condition, bool):
        return (lambda work: work()) if condition else (lambda work: None)
    return pl.when(condition)


def relay_kernel(
    chips,
    sections,
    in_flight,
    arriving,
    norm_gain,
    gate_up,
    w_down,
    expert_ids,
    route_weights,
    out,
    rows,
    cards,
    card_in,
    sum_in,
    sum_out,
    part_out,
    part_in,
    own,
    home,
    home_before,
    home_mate,
    inflow,
    entering,
    sum_before,
    sum_last,
    first,
    last,
    hidden,
    shares,
    gain,
    up_weights,
    down_weights,
    ids,
    weights,
    load_sems,
    swap_send,
    swap_recv,
    row_send,
    row_recv,
    mate_send,
    mate_recv,
    card_send,
    card_recv,
    card_mate_send,
    card_mate_recv,
    sum_send,
    sum_recv,
    part_send,
    part_recv,
    home_send,
    home_recv,
    before_send,
    before_recv,
    last_send,
    last_recv,
    out_send,
    out_recv,
    out_sems,
):
    steps, micros, top_count, tokens = expert_ids.shape[0], *expert_ids.shape[2:]
    features = in_flight.shape[-1]
    ff = w_down.shape[2]
    group = 2 * tokens
    tile = min(256, ff)
    experts = 2 * chips
    mine, other, block = pl.ds(0, tokens), pl.ds(tokens, tokens), pl.ds(0, group)
    chunks = [pl.ds(start, CHUNK) for start in range(0, group, CHUNK)]
    half = len(chunks) // 2

    me = lax.axis_index("expert")
    section = lax.axis_index("section")
    chip, core = me // 2, lax.rem(me, 2)
    mate = me + 1 - 2 * core
    role = lax.rem(core + chip, 2)

    def on_ring(distance):
        there = lax.rem(chip + distance * (1 - 2 * role) + chips, chips)
        return 2 * there + lax.rem(role + there, 2)

    ahead, behind = on_ring(1), on_ring(-1)
    ahead_mate = ahead + 1 - 2 * lax.rem(ahead, 2)
    has_after, has_before = section < sections - 1, section > 0
    section_after, section_before = section + 1, section - 1

    barrier = pltpu.get_barrier_semaphore()

    def greet(where):
        pl.semaphore_signal(barrier, inc=1, device_id=where, device_id_type=MESH)

    for device in (mate, behind, ahead_mate):
        greet({"expert": device})

    @pl.when(has_before)
    def _():
        greet({"section": section_before})
        greet({"section": section_before, "expert": behind})

    loads = [
        pltpu.make_async_copy(source, target, load_sems.at[i])
        for i, (source, target) in enumerate(
            (
                (in_flight.at[0, role], inflow.at[0, mine]),
                (norm_gain, gain),
                (expert_ids, ids),
                (route_weights, weights),
                (arriving.at[0, role], entering.at[mine]),
                (gate_up.at[0, 0], up_weights),
                (w_down.at[0, 0], down_weights),
            )
        )
    ]
    for load in loads:
        load.start()

    def normalize(step, rows_now):
        wide = inflow[step, rows_now].astype(jnp.float32)
        inverse = lax.rsqrt(jnp.mean(wide * wide, axis=-1, keepdims=True) + 1e-06)
        rows[step, 0, rows_now] = (wide * inverse * gain[...]).astype(jnp.bfloat16)

    pl.semaphore_wait(barrier, 3 + 2 * has_after.astype(jnp.int32))

    def swap(index, source, target):
        return pltpu.make_async_remote_copy(
            source, target, swap_send.at[index], swap_recv.at[index], {"expert": mate}, MESH
        )

    swaps = (
        swap(0, in_flight.at[0, 1 - role], inflow.at[0, other]),
        swap(1, shares.at[1 - role], card_in),
        swap(2, arriving.at[0, 1 - role], entering.at[other]),
    )
    swaps[0].start()


    loads[0].wait()
    loads[1].wait()
    normalize(0, mine)

    card_lane = lax.broadcasted_iota(jnp.int32, (tokens, LANES), 1)

    home_on = pltpu.make_async_remote_copy(
        home.at[0], home_before, home_send.at[0], home_recv.at[0], {"section": section_after}, MESH
    )
    home_over = pltpu.make_async_remote_copy(
        home.at[1, other], home_mate, home_send.at[1], home_recv.at[1], {"expert": mate}, MESH
    )

    def sum_to_next_section(i):
        return pltpu.make_async_remote_copy(
            sum_out.at[0, chips - 1, chunks[i]],
            sum_before.at[chunks[i]],
            before_send,
            before_recv.at[i],
            {"section": section_after, "expert": ahead},
            MESH,
        )

    def sum_to_owner(i, micro=role):
        return pltpu.make_async_remote_copy(
            sum_out.at[1, chips - 1, chunks[i]],
            sum_last.at[micro, chunks[i % half]],
            last_send,
            last_recv.at[micro, i % half],
            {"expert": ahead if i < half else ahead_mate},
            MESH,
        )

    def card_on(k):
        return pltpu.make_async_remote_copy(
            cards.at[k, mine], cards.at[k + 1, mine], card_send, card_recv.at[k + 1], {"expert": ahead}, MESH
        )

    def card_to_mate(k):
        return pltpu.make_async_remote_copy(
            cards.at[k, mine], cards.at[k, other], card_mate_send, card_mate_recv.at[k], {"expert": mate}, MESH
        )

    def make_cards():
        loads[2].wait()
        loads[3].wait()
        line = lax.broadcasted_iota(jnp.int32, (LANES, tokens), 0)
        for micro in range(micros):
            dense = []
            for step in range(steps):
                step_ids, step_weights = ids[step, 0, micro], weights[step, 0, micro]
                total = jnp.zeros((LANES, tokens), jnp.float32)
                for k in range(top_count):
                    named = step_ids[k : k + 1] == lax.rem(line, experts)
                    total = total + jnp.where(named, step_weights[k : k + 1], 0.0)
                dense.append(total)
            both = jnp.where(lax.rem(line, 2 * experts) < experts, dense[0], dense[1])
            side = line // (2 * experts)
            both = jnp.where(side == jnp.where(role == micro, 0, 1), both, 0.0)
            shares[micro] = both.T.astype(jnp.bfloat16)
        swaps[1].start()

    def relay_step(step):
        def pass_on(k, i):
            return pltpu.make_async_remote_copy(
                rows.at[step, k, chunks[i]],
                rows.at[step, k + 1, chunks[i]],
                row_send.at[step],
                row_recv.at[step, k + 1, i],
                {"expert": ahead},
                MESH,
            )

        def to_mate(k, i):
            return pltpu.make_async_remote_copy(
                rows.at[step, k, chunks[i]],
                rows.at[step, k, pl.ds(group + i * CHUNK, CHUNK)],
                mate_send.at[step],
                mate_recv.at[step, k],
                {"expert": mate},
                MESH,
            )

        def part_to_mate(k):
            return pltpu.make_async_remote_copy(
                part_out.at[step, k],
                part_in.at[step, k],
                part_send.at[step],
                part_recv.at[step, k],
                {"expert": mate},
                MESH,
            )

        def sum_on(k, i):
            return pltpu.make_async_remote_copy(
                sum_out.at[step, k, chunks[i]],
                sum_in.at[step, k + 1, chunks[i]],
                sum_send.at[step],
                sum_recv.at[step, k + 1, i],
                {"expert": ahead},
                MESH,
            )

        def forward(k, i):
            pass_on(k - 1, i).wait_recv()

            @pl.when(k < chips - 1)
            def _():
                pass_on(k, i).start()

            to_mate(k, i).start()
            if step == 0 and i == len(chunks) - 1:
                card_on(k - 1).wait_recv()

                @pl.when(k < chips - 1)
                def _():
                    card_on(k).start()

                card_to_mate(k).start()

        def multiply_up(k):
            arrived = rows.at[step, k, pl.ds(group, group)]
            pltpu.make_async_copy(arrived, arrived, mate_recv.at[step, k]).wait()
            both = rows[step, k]
            for start in range(0, ff, tile):
                gate = jnp.dot(
                    both, up_weights[:, start : start + tile], preferred_element_type=jnp.float32
                )
                lift = jnp.dot(
                    both,
                    up_weights[:, ff + start : ff + start + tile],
                    preferred_element_type=jnp.float32,
                )
                hidden[:, start : start + tile] = (gate / (1.0 + jnp.exp(-gate)) * lift).astype(
                    jnp.bfloat16
                )

        def multiply_down(k):
            slot = lax.rem(k, 2)
            if step == 0:
                card_to_mate(k).wait_recv()
            at = step * experts + me
            share = []
            for card_rows in (mine, other):
                card = cards[k, card_rows].astype(jnp.float32)
                for lane in (at, at + 2 * experts):
                    picked = jnp.where(card_lane == lane, card, 0.0)
                    share.append(jnp.sum(picked, axis=1, keepdims=True))
            share = jnp.concatenate(share, axis=0)
            for start in range(0, features, tile):
                result = jnp.dot(
                    hidden[...],
                    down_weights[:, start : start + tile],
                    preferred_element_type=jnp.float32,
                )
                result = result.astype(jnp.bfloat16).astype(jnp.float32) * share
                own[slot, :, start : start + tile] = result[:group]
                part_out[step, k, :, start : start + tile] = result[group:].astype(jnp.bfloat16)
            part_to_mate(k).start()

        def add(k, i):
            @pl.when(k > 1)
            def _():
                sum_on(k - 1, i).wait_recv()

            rows_now = chunks[i]
            total = own[lax.rem(k, 2), rows_now] + part_in[step, k, rows_now].astype(jnp.float32)
            total = total + sum_in[step, k, rows_now].astype(jnp.float32)
            sum_out[step, k, rows_now] = total.astype(jnp.bfloat16)

        def add_on(k, i):
            add(k, i)
            sum_on(k, i).start()

        def take_part(k):
            part_to_mate(k).wait_recv()

            @when(k == 0)
            def _():
                home[step] = (
                    own[0]
                    + part_in[step, 0].astype(jnp.float32)
                    + inflow[step].astype(jnp.float32)
                )
                if step == 0:

                    @pl.when(has_after)
                    def _():
                        home_on.start()

                else:
                    home_over.start()

        def finish(i):
            add(chips - 1, i)
            if step == 0:

                @pl.when(has_after)
                def _():
                    sum_to_next_section(i).start()

            else:
                sum_to_owner(i).start()

        def turn(k):
            for what, behind_by, i in TURN:
                b = k - behind_by
                if isinstance(b, int) and not 0 <= b < chips:
                    continue
                if what == "row":
                    if not isinstance(b, int) or b > 0:
                        forward(b, i)
                elif what == "up":
                    when(b >= 0)(functools.partial(multiply_up, b))
                elif what == "down":
                    when(b >= 0)(functools.partial(multiply_down, b))
                elif what == "part":
                    when(b >= 0)(functools.partial(take_part, b))
                elif isinstance(b, int) and b == chips - 1:
                    finish(i)
                else:
                    when(b > 0)(functools.partial(add_on, b, i))

        for i, rows_now in enumerate(chunks):
            if step == 0 and i == half:
                make_cards()
                swaps[0].wait_recv()
                normalize(0, other)
            if step == 1:
                if i == 0:

                    @pl.when(has_before)
                    def _():
                        home_on.wait_recv()

                @pl.when(has_before)
                def _():
                    sum_to_next_section(i).wait_recv()
                    total = home_before[rows_now] + sum_before[rows_now].astype(jnp.float32)
                    inflow[1, rows_now] = total.astype(jnp.bfloat16)

                @pl.when(section == 0)
                def _():
                    inflow[1, rows_now] = entering[rows_now]

                normalize(1, rows_now)
            pass_on(0, i).start()
            to_mate(0, i).start()
        if step == 0:
            swaps[1].wait_recv()
            cards[0, mine] = shares[role] + card_in[...]
            card_on(0).start()
            card_to_mate(0).start()
            swaps[2].start()
            sum_in[:, 1] = jnp.zeros((steps,) + sum_in.shape[2:], sum_in.dtype)
            loads[5].wait()
            loads[6].wait()
        turn(0)
        pl.loop(1, chips)(turn)
        for k in range(chips, chips + 1 + max(behind_by for _, behind_by, _ in TURN)):
            turn(k)
        if step == 0:
            for i in range(len(chunks)):
                sum_on(chips - 1, i).start()
            loads[4].wait()
            swaps[2].wait_recv()

    relay_step(0)

    def first_out():
        return (
            pltpu.make_async_copy(first.at[mine], out.at[0, 0, role], out_sems.at[0]),
            pltpu.make_async_remote_copy(
                first.at[other], out.at[0, 0, role], out_send, out_recv, {"expert": mate}, MESH
            ),
        )

    relay_step(1)

    for i, rows_now in enumerate(chunks):
        come_round = sum_in.at[0, chips, rows_now]
        pltpu.make_async_copy(come_round, come_round, sum_recv.at[0, chips, i]).wait()
        first[rows_now] = (home[0, rows_now] + come_round[...].astype(jnp.float32)).astype(
            jnp.bfloat16
        )
    for copy in first_out():
        copy.start()

    home_over.wait_recv()
    for i in range(half):
        sum_to_owner(i).wait_recv()
        total = home[1, chunks[i]] + sum_last[role, chunks[i]].astype(jnp.float32)
        last[role, chunks[i]] = total.astype(jnp.bfloat16)
    for i in range(half):
        sum_to_owner(i, 1 - role).wait_recv()
        total = home_mate[chunks[i]] + sum_last[1 - role, chunks[i]].astype(jnp.float32)
        last[1 - role, chunks[i]] = total.astype(jnp.bfloat16)
    last_out = pltpu.make_async_copy(last, out.at[1, 0], out_sems.at[1])
    last_out.start()

    def drain(source, sem):
        pltpu.make_async_copy(source, source, sem).wait()

    for copy in swaps:
        copy.wait_send()

    @pl.when(has_after)
    def _():
        home_on.wait_send()
        drain(sum_out.at[0, chips - 1], before_send)

    home_over.wait_send()
    drain(sum_out.at[1, chips - 1], last_send)
    drain(cards.at[pl.ds(0, chips - 1), mine], card_send)
    drain(cards.at[pl.ds(0, chips), mine], card_mate_send)
    for step in range(steps):
        drain(rows.at[step, pl.ds(0, chips - 1), block], row_send.at[step])
        drain(rows.at[step, pl.ds(0, chips), block], mate_send.at[step])
        drain(part_out.at[step], part_send.at[step])
        sums = pl.ds(1, chips - 1 - step)
        drain(sum_out.at[step, sums], sum_send.at[step])
    for copy in first_out():
        copy.wait()
    last_out.wait()


def local(in_flight, arriving, norm_gain, gate_up, w_down, expert_ids, route_weights):
    sections, chips = lax.axis_size("section"), lax.axis_size("expert") // 2
    _, micros, tokens, features = in_flight.shape
    steps = expert_ids.shape[0]
    ff = w_down.shape[2]
    group = 2 * tokens
    pieces = group // CHUNK
    expert_ids, route_weights = expert_ids.swapaxes(3, 4), route_weights.swapaxes(3, 4)
    half, full = jnp.bfloat16, jnp.float32
    dma = pltpu.SemaphoreType.DMA
    block = (group, features)
    anywhere = pl.BlockSpec(memory_space=pl.ANY)
    return pl.pallas_call(
        functools.partial(relay_kernel, chips, sections),
        out_shape=pltpu.VMEM((steps, 1, micros, tokens, features), half),
        in_specs=[anywhere] * 7,
        out_specs=pl.BlockSpec(memory_space=pltpu.VMEM),
        scratch_shapes=[
            pltpu.VMEM((steps, chips, 2 * group, features), half),
            pltpu.VMEM((chips, group, LANES), half),
            pltpu.VMEM((tokens, LANES), half),
            pltpu.VMEM((steps, chips + 1) + block, half),
            pltpu.VMEM((steps, chips) + block, half),
            pltpu.VMEM((steps, chips) + block, half),
            pltpu.VMEM((steps, chips) + block, half),
            pltpu.VMEM((2,) + block, full),
            pltpu.VMEM((steps,) + block, full),
            pltpu.VMEM(block, full),
            pltpu.VMEM((tokens, features), full),
            pltpu.VMEM((steps,) + block, half),
            pltpu.VMEM(block, half),
            pltpu.VMEM(block, half),
            pltpu.VMEM((micros, tokens, features), half),
            pltpu.VMEM(block, half),
            pltpu.VMEM((micros, tokens, features), half),
            pltpu.VMEM((2 * group, ff), half),
            pltpu.VMEM((micros, tokens, LANES), half),
            pltpu.VMEM((1, features), full),
            pltpu.VMEM(gate_up.shape[2:], half),
            pltpu.VMEM(w_down.shape[2:], half),
            pltpu.VMEM(expert_ids.shape, jnp.int32),
            pltpu.VMEM(route_weights.shape, full),
            dma((7,)),
            dma((3,)),
            dma((3,)),
            dma((steps,)),
            dma((steps, chips, pieces)),
            dma((steps,)),
            dma((steps, chips)),
            dma,
            dma((chips,)),
            dma,
            dma((chips,)),
            dma((steps,)),
            dma((steps, chips + 1, pieces)),
            dma((steps,)),
            dma((steps, chips)),
            dma((2,)),
            dma((2,)),
            dma,
            dma((pieces,)),
            dma,
            dma((micros, pieces // 2)),
            dma,
            dma,
            dma((steps,)),
        ],
        compiler_params=pltpu.CompilerParams(
            collective_id=0, has_side_effects=True, vmem_limit_bytes=56 * 2**20
        ),
        name="relay",
    )(in_flight, arriving, norm_gain, gate_up, w_down, expert_ids, route_weights)


def solution(mesh):
    return jax.shard_map(
        local,
        mesh=mesh,
        in_specs=(
            P("section", None, "expert", None),
            P(None, None, "expert", None),
            P("section", None),
            P("section", "expert", None, None),
            P("section", "expert", None, None),
            P(None, "section", None, "expert", None),
            P(None, "section", None, "expert", None),
        ),
        out_specs=P(None, "section", None, "expert", None),
        check_vma=False,
    )
```

```python
import functools

import jax
import jax.numpy as jnp
from jax import lax
from jax.experimental import pallas as pl
from jax.experimental.pallas import tpu as pltpu
from jax.sharding import PartitionSpec as P

MESH = pl.DeviceIdType.MESH
LANES = 128
CHUNK = 16
TURN = (
    ("row", 0, 0),
    ("sum", 2, 3),
    ("down", 1, 0),
    ("row", 0, 1),
    ("row", 0, 2),
    ("row", 0, 3),
    ("part", 1, 0),
    ("sum", 1, 0),
    ("sum", 1, 1),
    ("sum", 1, 2),
    ("up", 0, 0),
)


def when(condition):
    if isinstance(condition, bool):
        return (lambda work: work()) if condition else (lambda work: None)
    return pl.when(condition)


def relay_kernel(
    chips,
    sections,
    in_flight,
    arriving,
    norm_gain,
    gate_up,
    w_down,
    expert_ids,
    route_weights,
    out,
    rows,
    cards,
    card_in,
    sum_in,
    sum_out,
    part_out,
    part_in,
    own,
    home,
    home_before,
    home_mate,
    inflow,
    entering,
    sum_before,
    sum_last,
    first,
    last,
    hidden,
    shares,
    gain,
    up_weights,
    down_weights,
    ids,
    weights,
    load_sems,
    swap_send,
    swap_recv,
    row_send,
    row_recv,
    mate_send,
    mate_recv,
    card_send,
    card_recv,
    card_mate_send,
    card_mate_recv,
    sum_send,
    sum_recv,
    part_send,
    part_recv,
    home_send,
    home_recv,
    before_send,
    before_recv,
    last_send,
    last_recv,
    out_send,
    out_recv,
    out_sems,
):
    steps, micros, top_count, tokens = expert_ids.shape[0], *expert_ids.shape[2:]
    features = in_flight.shape[-1]
    ff = w_down.shape[2]
    group = 2 * tokens
    tile = min(256, ff)
    experts = 2 * chips
    mine, other, block = pl.ds(0, tokens), pl.ds(tokens, tokens), pl.ds(0, group)
    chunks = [pl.ds(start, CHUNK) for start in range(0, group, CHUNK)]
    half = len(chunks) // 2

    me = lax.axis_index("expert")
    section = lax.axis_index("section")
    chip, core = me // 2, lax.rem(me, 2)
    mate = me + 1 - 2 * core
    role = lax.rem(core + chip, 2)

    def on_ring(distance):
        there = lax.rem(chip + distance * (1 - 2 * role) + chips, chips)
        return 2 * there + lax.rem(role + there, 2)

    ahead, behind = on_ring(1), on_ring(-1)
    ahead_mate = ahead + 1 - 2 * lax.rem(ahead, 2)
    has_after, has_before = section < sections - 1, section > 0
    section_after, section_before = section + 1, section - 1

    barrier = pltpu.get_barrier_semaphore()

    def greet(where):
        pl.semaphore_signal(barrier, inc=1, device_id=where, device_id_type=MESH)

    for device in (mate, behind, ahead_mate):
        greet({"expert": device})

    @pl.when(has_before)
    def _():
        greet({"section": section_before})
        greet({"section": section_before, "expert": behind})

    loads = [
        pltpu.make_async_copy(source, target, load_sems.at[i])
        for i, (source, target) in enumerate(
            (
                (in_flight.at[0, role], inflow.at[0, mine]),
                (norm_gain, gain),
                (expert_ids, ids),
                (route_weights, weights),
                (arriving.at[0, role], entering.at[mine]),
                (gate_up.at[0, 0], up_weights),
                (w_down.at[0, 0], down_weights),
            )
        )
    ]
    for load in loads:
        load.start()

    def normalize(step, rows_now):
        wide = inflow[step, rows_now].astype(jnp.float32)
        inverse = lax.rsqrt(jnp.mean(wide * wide, axis=-1, keepdims=True) + 1e-06)
        rows[step, 0, rows_now] = (wide * inverse * gain[...]).astype(jnp.bfloat16)

    pl.semaphore_wait(barrier, 3 + 2 * has_after.astype(jnp.int32))

    def swap(index, source, target):
        return pltpu.make_async_remote_copy(
            source, target, swap_send.at[index], swap_recv.at[index], {"expert": mate}, MESH
        )

    swaps = (
        swap(0, in_flight.at[0, 1 - role], inflow.at[0, other]),
        swap(1, shares.at[1 - role], card_in),
        swap(2, arriving.at[0, 1 - role], entering.at[other]),
    )
    swaps[0].start()


    loads[0].wait()
    loads[1].wait()
    normalize(0, mine)

    card_lane = lax.broadcasted_iota(jnp.int32, (tokens, LANES), 1)

    home_on = pltpu.make_async_remote_copy(
        home.at[0], home_before, home_send.at[0], home_recv.at[0], {"section": section_after}, MESH
    )
    home_over = pltpu.make_async_remote_copy(
        home.at[1, other], home_mate, home_send.at[1], home_recv.at[1], {"expert": mate}, MESH
    )

    def sum_to_next_section(i):
        return pltpu.make_async_remote_copy(
            sum_out.at[0, chips - 1, chunks[i]],
            sum_before.at[chunks[i]],
            before_send,
            before_recv.at[i],
            {"section": section_after, "expert": ahead},
            MESH,
        )

    def sum_to_owner(i, micro=role):
        return pltpu.make_async_remote_copy(
            sum_out.at[1, chips - 1, chunks[i]],
            sum_last.at[micro, chunks[i % half]],
            last_send,
            last_recv.at[micro, i % half],
            {"expert": ahead if i < half else ahead_mate},
            MESH,
        )

    def card_on(k):
        return pltpu.make_async_remote_copy(
            cards.at[k, mine], cards.at[k + 1, mine], card_send, card_recv.at[k + 1], {"expert": ahead}, MESH
        )

    def card_to_mate(k):
        return pltpu.make_async_remote_copy(
            cards.at[k, mine], cards.at[k, other], card_mate_send, card_mate_recv.at[k], {"expert": mate}, MESH
        )

    def make_cards():
        loads[2].wait()
        loads[3].wait()
        line = lax.broadcasted_iota(jnp.int32, (LANES, tokens), 0)
        for micro in range(micros):
            dense = []
            for step in range(steps):
                step_ids, step_weights = ids[step, 0, micro], weights[step, 0, micro]
                total = jnp.zeros((LANES, tokens), jnp.float32)
                for k in range(top_count):
                    named = step_ids[k : k + 1] == lax.rem(line, experts)
                    total = total + jnp.where(named, step_weights[k : k + 1], 0.0)
                dense.append(total)
            both = jnp.where(lax.rem(line, 2 * experts) < experts, dense[0], dense[1])
            side = line // (2 * experts)
            both = jnp.where(side == jnp.where(role == micro, 0, 1), both, 0.0)
            shares[micro] = both.T.astype(jnp.bfloat16)
        swaps[1].start()

    def come_home():
        return pltpu.make_async_remote_copy(
            sum_out.at[0, chips - 1],
            sum_in.at[0, chips],
            sum_send.at[0],
            sum_recv.at[0, chips, 0],
            {"expert": ahead},
            MESH,
        )

    def relay_step(step):
        def pass_on(k, i):
            return pltpu.make_async_remote_copy(
                rows.at[step, k, chunks[i]],
                rows.at[step, k + 1, chunks[i]],
                row_send.at[step],
                row_recv.at[step, k + 1, i],
                {"expert": ahead},
                MESH,
            )

        def to_mate(k, i):
            return pltpu.make_async_remote_copy(
                rows.at[step, k, chunks[i]],
                rows.at[step, k, pl.ds(group + i * CHUNK, CHUNK)],
                mate_send.at[step],
                mate_recv.at[step, k],
                {"expert": mate},
                MESH,
            )

        def part_to_mate(k):
            return pltpu.make_async_remote_copy(
                part_out.at[step, k],
                part_in.at[step, k],
                part_send.at[step],
                part_recv.at[step, k],
                {"expert": mate},
                MESH,
            )

        def sum_on(k, i):
            return pltpu.make_async_remote_copy(
                sum_out.at[step, k, chunks[i]],
                sum_in.at[step, k + 1, chunks[i]],
                sum_send.at[step],
                sum_recv.at[step, k + 1, i],
                {"expert": ahead},
                MESH,
            )

        def forward(k, i):
            pass_on(k - 1, i).wait_recv()

            @pl.when(k < chips - 1)
            def _():
                pass_on(k, i).start()

            to_mate(k, i).start()
            if step == 0 and i == len(chunks) - 1:
                card_on(k - 1).wait_recv()

                @pl.when(k < chips - 1)
                def _():
                    card_on(k).start()

                card_to_mate(k).start()

        def multiply_up(k):
            arrived = rows.at[step, k, pl.ds(group, group)]
            pltpu.make_async_copy(arrived, arrived, mate_recv.at[step, k]).wait()
            both = rows[step, k]
            for start in range(0, ff, ff):
                gate = jnp.dot(
                    both, up_weights[:, start : start + ff], preferred_element_type=jnp.float32
                )
                lift = jnp.dot(
                    both,
                    up_weights[:, ff + start : ff + start + ff],
                    preferred_element_type=jnp.float32,
                )
                hidden[:, start : start + ff] = (gate / (1.0 + jnp.exp(-gate)) * lift).astype(
                    jnp.bfloat16
                )

        def multiply_down(k):
            slot = lax.rem(k, 2)
            if step == 0:
                card_to_mate(k).wait_recv()
            at = step * experts + me
            share = []
            for card_rows in (mine, other):
                card = cards[k, card_rows].astype(jnp.float32)
                for lane in (at, at + 2 * experts):
                    picked = jnp.where(card_lane == lane, card, 0.0)
                    share.append(jnp.sum(picked, axis=1, keepdims=True))
            share = jnp.concatenate(share, axis=0)
            for start in range(0, features, tile):
                result = jnp.dot(
                    hidden[...],
                    down_weights[:, start : start + tile],
                    preferred_element_type=jnp.float32,
                )
                result = result.astype(jnp.bfloat16).astype(jnp.float32) * share
                own[slot, :, start : start + tile] = result[:group]
                part_out[step, k, :, start : start + tile] = result[group:].astype(jnp.bfloat16)
            part_to_mate(k).start()

        def add(k, i):
            @pl.when(k > 1)
            def _():
                sum_on(k - 1, i).wait_recv()

            rows_now = chunks[i]
            total = own[lax.rem(k, 2), rows_now] + part_in[step, k, rows_now].astype(jnp.float32)
            total = total + sum_in[step, k, rows_now].astype(jnp.float32)
            sum_out[step, k, rows_now] = total.astype(jnp.bfloat16)

        def add_on(k, i):
            add(k, i)
            sum_on(k, i).start()

        def take_part(k):
            part_to_mate(k).wait_recv()

            @when(k == 0)
            def _():
                home[step] = (
                    own[0]
                    + part_in[step, 0].astype(jnp.float32)
                    + inflow[step].astype(jnp.float32)
                )
                if step == 0:

                    @pl.when(has_after)
                    def _():
                        home_on.start()

                else:
                    home_over.start()

        def finish(i):
            add(chips - 1, i)
            if step == 0:

                @pl.when(has_after)
                def _():
                    sum_to_next_section(i).start()

            else:
                sum_to_owner(i).start()

        def turn(k):
            for what, behind_by, i in TURN:
                b = k - behind_by
                if isinstance(b, int) and not 0 <= b < chips:
                    continue
                if what == "row":
                    if not isinstance(b, int) or b > 0:
                        forward(b, i)
                elif what == "up":
                    when(b >= 0)(functools.partial(multiply_up, b))
                elif what == "down":
                    when(b >= 0)(functools.partial(multiply_down, b))
                elif what == "part":
                    when(b >= 0)(functools.partial(take_part, b))
                elif isinstance(b, int) and b == chips - 1:
                    finish(i)
                else:
                    when(b > 0)(functools.partial(add_on, b, i))

        for i, rows_now in enumerate(chunks):
            if step == 0 and i == half:
                make_cards()
                swaps[0].wait_recv()
                normalize(0, other)
            if step == 1:
                if i == 0:

                    @pl.when(has_before)
                    def _():
                        home_on.wait_recv()

                @pl.when(has_before)
                def _():
                    sum_to_next_section(i).wait_recv()
                    total = home_before[rows_now] + sum_before[rows_now].astype(jnp.float32)
                    inflow[1, rows_now] = total.astype(jnp.bfloat16)

                @pl.when(section == 0)
                def _():
                    inflow[1, rows_now] = entering[rows_now]

                normalize(1, rows_now)
            pass_on(0, i).start()
            to_mate(0, i).start()
        if step == 1:
            come_home().start()
        if step == 0:
            swaps[1].wait_recv()
            cards[0, mine] = shares[role] + card_in[...]
            card_on(0).start()
            card_to_mate(0).start()
            swaps[2].start()
            sum_in[:, 1] = jnp.zeros((steps,) + sum_in.shape[2:], sum_in.dtype)
            loads[5].wait()
            loads[6].wait()
        turn(0)
        pl.loop(1, chips)(turn)
        for k in range(chips, chips + 1 + max(behind_by for _, behind_by, _ in TURN)):
            turn(k)
        if step == 0:
            loads[4].wait()
            swaps[2].wait_recv()

    relay_step(0)

    def first_out():
        return (
            pltpu.make_async_copy(first.at[mine], out.at[0, 0, role], out_sems.at[0]),
            pltpu.make_async_remote_copy(
                first.at[other], out.at[0, 0, role], out_send, out_recv, {"expert": mate}, MESH
            ),
        )

    relay_step(1)

    come_home().wait_recv()
    for rows_now in chunks:
        come_round = sum_in.at[0, chips, rows_now]
        first[rows_now] = (home[0, rows_now] + come_round[...].astype(jnp.float32)).astype(
            jnp.bfloat16
        )
    for copy in first_out():
        copy.start()

    home_over.wait_recv()
    for i in range(half):
        sum_to_owner(i).wait_recv()
        total = home[1, chunks[i]] + sum_last[role, chunks[i]].astype(jnp.float32)
        last[role, chunks[i]] = total.astype(jnp.bfloat16)
    for i in range(half):
        sum_to_owner(i, 1 - role).wait_recv()
        total = home_mate[chunks[i]] + sum_last[1 - role, chunks[i]].astype(jnp.float32)
        last[1 - role, chunks[i]] = total.astype(jnp.bfloat16)
    last_out = pltpu.make_async_copy(last, out.at[1, 0], out_sems.at[1])
    last_out.start()

    def drain(source, sem):
        pltpu.make_async_copy(source, source, sem).wait()

    for copy in swaps:
        copy.wait_send()

    @pl.when(has_after)
    def _():
        home_on.wait_send()
        drain(sum_out.at[0, chips - 1], before_send)

    home_over.wait_send()
    drain(sum_out.at[1, chips - 1], last_send)
    drain(cards.at[pl.ds(0, chips - 1), mine], card_send)
    drain(cards.at[pl.ds(0, chips), mine], card_mate_send)
    for step in range(steps):
        drain(rows.at[step, pl.ds(0, chips - 1), block], row_send.at[step])
        drain(rows.at[step, pl.ds(0, chips), block], mate_send.at[step])
        drain(part_out.at[step], part_send.at[step])
        sums = pl.ds(1, chips - 1 - step)
        drain(sum_out.at[step, sums], sum_send.at[step])
    for copy in first_out():
        copy.wait()
    last_out.wait()


def local(in_flight, arriving, norm_gain, gate_up, w_down, expert_ids, route_weights):
    sections, chips = lax.axis_size("section"), lax.axis_size("expert") // 2
    _, micros, tokens, features = in_flight.shape
    steps = expert_ids.shape[0]
    ff = w_down.shape[2]
    group = 2 * tokens
    pieces = group // CHUNK
    expert_ids, route_weights = expert_ids.swapaxes(3, 4), route_weights.swapaxes(3, 4)
    half, full = jnp.bfloat16, jnp.float32
    dma = pltpu.SemaphoreType.DMA
    block = (group, features)
    anywhere = pl.BlockSpec(memory_space=pl.ANY)
    return pl.pallas_call(
        functools.partial(relay_kernel, chips, sections),
        out_shape=pltpu.VMEM((steps, 1, micros, tokens, features), half),
        in_specs=[anywhere] * 7,
        out_specs=pl.BlockSpec(memory_space=pltpu.VMEM),
        scratch_shapes=[
            pltpu.VMEM((steps, chips, 2 * group, features), half),
            pltpu.VMEM((chips, group, LANES), half),
            pltpu.VMEM((tokens, LANES), half),
            pltpu.VMEM((steps, chips + 1) + block, half),
            pltpu.VMEM((steps, chips) + block, half),
            pltpu.VMEM((steps, chips) + block, half),
            pltpu.VMEM((steps, chips) + block, half),
            pltpu.VMEM((2,) + block, full),
            pltpu.VMEM((steps,) + block, full),
            pltpu.VMEM(block, full),
            pltpu.VMEM((tokens, features), full),
            pltpu.VMEM((steps,) + block, half),
            pltpu.VMEM(block, half),
            pltpu.VMEM(block, half),
            pltpu.VMEM((micros, tokens, features), half),
            pltpu.VMEM(block, half),
            pltpu.VMEM((micros, tokens, features), half),
            pltpu.VMEM((2 * group, ff), half),
            pltpu.VMEM((micros, tokens, LANES), half),
            pltpu.VMEM((1, features), full),
            pltpu.VMEM(gate_up.shape[2:], half),
            pltpu.VMEM(w_down.shape[2:], half),
            pltpu.VMEM(expert_ids.shape, jnp.int32),
            pltpu.VMEM(route_weights.shape, full),
            dma((7,)),
            dma((3,)),
            dma((3,)),
            dma((steps,)),
            dma((steps, chips, pieces)),
            dma((steps,)),
            dma((steps, chips)),
            dma,
            dma((chips,)),
            dma,
            dma((chips,)),
            dma((steps,)),
            dma((steps, chips + 1, pieces)),
            dma((steps,)),
            dma((steps, chips)),
            dma((2,)),
            dma((2,)),
            dma,
            dma((pieces,)),
            dma,
            dma((micros, pieces // 2)),
            dma,
            dma,
            dma((steps,)),
        ],
        compiler_params=pltpu.CompilerParams(
            collective_id=0, has_side_effects=True, vmem_limit_bytes=56 * 2**20
        ),
        name="relay",
    )(in_flight, arriving, norm_gain, gate_up, w_down, expert_ids, route_weights)


def solution(mesh):
    return jax.shard_map(
        local,
        mesh=mesh,
        in_specs=(
            P("section", None, "expert", None),
            P(None, None, "expert", None),
            P("section", None),
            P("section", "expert", None, None),
            P("section", "expert", None, None),
            P(None, "section", None, "expert", None),
            P(None, "section", None, "expert", None),
        ),
        out_specs=P(None, "section", None, "expert", None),
        check_vma=False,
    )
```
